32 devices in a mesh: table: 8 (over z, core), dp: 4 (over y, x).
Axes of the slice: x: 2, y: 2, z: 4, core: 2. Of those that a mesh axis runs over, the one named last changes fastest.
Arguments:
- ids: int32 [8, 512, 128], P('table', 'dp'), may hold values from 0 to 1023
- mults: int32 [8, 512, 128], P('table', 'dp'), may hold values from 0 to 2
- table: bfloat16 [8192, 128], P('table'), may hold values from -1.25 to 1.25
- user_layer: bfloat16 [1024, 512], replicated, may hold values from -0.1875 to 0.1875
- user_head: bfloat16 [512, 128], replicated, may hold values from -0.25 to 0.25
- item_layer: bfloat16 [1024, 512], replicated, may hold values from -0.1875 to 0.1875
- item_head: bfloat16 [512, 128], replicated, may hold values from -0.25 to 0.25
- counts: int32 [4, 128], P('dp', 'table'), may hold values from 1 to 256
Outputs:
- losses: float32 [4, 128], P('dp', 'table')
- table_change: float32 [8192, 128], P('table')
- user_layer_change: float32 [1024, 512], P('table')
- user_head_change: float32 [512, 128], P('table')
- item_layer_change: float32 [1024, 512], P('table')
- item_head_change: float32 [512, 128], P('table')
The draws below stay inside these ranges and needn't reach their ends.
All inputs are finite; a program needn't handle non-finite values.
Results may differ from the reference program's by a relative error of at most 0.039.
Values may be sent and summed in bfloat16 or wider, within the bound.
A program may use at most 64 MiB of HBM per device.

```python
import jax
import jax.numpy as jnp
from jax import lax

EMB = 128
F_USER = 8
F_ITEM = 8
HID = 512
OUT = 128
LOOKUPS = 8
R_DEV = 1024
B_DEV = 16
BATCH = 512
N_TABLE = 8
N_DP = 4


def plant(entries, rng, smallest, top_value):
    index_at = [jax.random.randint(jax.random.fold_in(rng, axis), (), 0, length) for axis, length in enumerate(entries.shape)]
    longest = entries.shape.index(max(entries.shape))
    beside = index_at[:longest] + [(index_at[longest] + 1) % entries.shape[longest]] + index_at[longest + 1:]
    return entries.at[tuple(index_at)].set(smallest).at[tuple(beside)].set(top_value)


def levels(rng, dims, cuts, low, high):
    gain = 1.0
    for axis_at, parts in cuts:
        heights = jax.random.uniform(jax.random.fold_in(jax.random.fold_in(rng, 6), axis_at), (parts,), jnp.float32, low / len(cuts), high / len(cuts))
        gain = gain * jnp.repeat(jnp.exp(heights), dims[axis_at] // parts).reshape((-1,) + (1,) * (len(dims) - 1 - axis_at))
    return gain


def noise(own_key, dims, deviation, limit, cuts=(), kind=jnp.bfloat16):
    entries = jax.random.normal(own_key, dims, jnp.float32) * deviation
    if len(cuts) > 0:
        entries = levels(own_key, dims, cuts, -0.22, 0.18) * entries
    return jnp.clip(entries, min=-limit, max=limit).astype(kind)


def setup_inputs(seed: int = 0) -> dict:
    key_of = jax.random.split(jax.random.key(seed), 9)
    ids = plant(jax.random.randint(key_of[0], (N_TABLE, BATCH, (F_USER + F_ITEM) * LOOKUPS), 0, R_DEV), jax.random.fold_in(key_of[0], 1), 0, R_DEV - 1).astype(jnp.int32)
    mults = plant(jax.random.randint(key_of[1], (N_TABLE, BATCH, (F_USER + F_ITEM) * LOOKUPS), 0, 3), jax.random.fold_in(key_of[1], 1), 0, 2).astype(jnp.int32)
    table = noise(key_of[2], (N_TABLE * R_DEV, EMB), ((2 * N_TABLE * LOOKUPS) ** -0.5), 1.25, ((0, 8),))
    user_layer = noise(key_of[3], (F_USER * EMB, HID), (F_USER * EMB) ** -0.5, 0.1875)
    user_head = noise(key_of[4], (HID, OUT), HID ** -0.5, 0.25)
    item_layer = noise(key_of[5], (F_ITEM * EMB, HID), (F_ITEM * EMB) ** -0.5, 0.1875)
    item_head = noise(key_of[6], (HID, OUT), HID ** -0.5, 0.25)
    counts = plant(jax.random.randint(key_of[7], (N_DP, N_TABLE * B_DEV), 1, 257), jax.random.fold_in(key_of[7], 1), 1, 256).astype(jnp.int32)
    return {"ids": ids, "mults": mults, "table": table, "user_layer": user_layer, "user_head": user_head, "item_layer": item_layer, "item_head": item_head, "counts": counts}


INVERSE_TEMP = 20.0
EPSILON = 1e-06

def silu_slope(pre):
    gate = jax.nn.sigmoid(pre)
    return gate * (1.0 + pre * (1.0 - gate))

def run_tower(pooled_in, layer, head):
    pre = jnp.dot(pooled_in, layer, preferred_element_type=jnp.float32)
    hidden = jax.nn.silu(pre).astype(jnp.bfloat16)
    output = jnp.dot(hidden, head, preferred_element_type=jnp.float32)
    return (pre, hidden, output)

def unit_scale(output):
    return lax.rsqrt(lax.optimization_barrier(jnp.sum(output * output, axis=-1, keepdims=True)) + EPSILON)

def tower_back(d_unit, output, pre, layer, head):
    scale = unit_scale(output)
    unit = output * scale
    along = lax.optimization_barrier(jnp.sum(unit * d_unit, axis=-1, keepdims=True))
    d_output = ((d_unit - unit * along) * scale).astype(jnp.bfloat16)
    d_hidden = (jnp.dot(d_output, head.T, preferred_element_type=jnp.float32) * silu_slope(pre)).astype(jnp.bfloat16)
    d_pooled = jnp.dot(d_hidden, layer.T, preferred_element_type=jnp.float32).astype(jnp.bfloat16)
    return (d_output, d_hidden, d_pooled)

def rounded_term(left, right):
    term = jnp.dot(left.T, right, preferred_element_type=jnp.float32).astype(jnp.bfloat16)
    return lax.optimization_barrier(term).astype(jnp.float32)

def reference(ids, mults, table, user_layer, user_head, item_layer, item_head, counts):
    feature_count = F_USER + F_ITEM
    group_rows = B_DEV * N_TABLE
    batch_rows = group_rows * N_DP
    shard_list = jnp.arange(N_TABLE, dtype=jnp.int32)

    def shard_inputs(shard):
        shard_ids = lax.dynamic_index_in_dim(ids, shard, 0, keepdims=False)
        shard_mults = lax.dynamic_index_in_dim(mults, shard, 0, keepdims=False)
        shape = (N_DP, group_rows, feature_count, LOOKUPS)
        return (shard_ids.reshape(shape).astype(jnp.int32), shard_mults.reshape(shape))

    def shard_pool(running, shard):
        rows = lax.dynamic_slice_in_dim(table, shard * R_DEV, R_DEV, 0).astype(jnp.float32)
        shard_ids, shard_mults = shard_inputs(shard)

        def block_pool(lookup_pair):
            picked = rows[lookup_pair[0]]
            return lax.optimization_barrier(jnp.sum(picked * lookup_pair[1].astype(jnp.float32)[..., None], axis=2)).astype(jnp.bfloat16)
        partial_value = lax.map(block_pool, (shard_ids, shard_mults))
        return (running + partial_value.astype(jnp.float32), None)
    summed, _ = lax.scan(shard_pool, jnp.zeros((N_DP, group_rows, feature_count, EMB), jnp.float32), shard_list)
    pooled = summed.astype(jnp.bfloat16).reshape(batch_rows, feature_count * EMB)
    user_width = F_USER * EMB
    user_in = pooled[:, :user_width]
    item_in = pooled[:, user_width:]
    user_pre, user_hidden, user_output = run_tower(user_in, user_layer, user_head)
    item_pre, item_hidden, item_output = run_tower(item_in, item_layer, item_head)
    user_unit = (user_output * unit_scale(user_output)).astype(jnp.bfloat16)
    item_unit = (item_output * unit_scale(item_output)).astype(jnp.bfloat16)

    def by_table(values):
        return values.reshape(N_DP, N_TABLE, B_DEV, -1).transpose(1, 0, 2, 3).reshape(N_TABLE, N_DP * B_DEV, -1)

    def by_batch(values):
        return values.reshape(N_TABLE, N_DP, B_DEV, -1).transpose(1, 0, 2, 3).reshape(batch_rows, -1)
    queries = by_table(user_unit).astype(jnp.float32)
    keys = by_table(item_unit).astype(jnp.float32)
    log_freq = by_table(jnp.log(counts.astype(jnp.float32)).reshape(batch_rows, 1))[..., 0]
    scores = INVERSE_TEMP * jnp.einsum('tik,tjk->tij', queries, keys) - log_freq[:, None, :]
    lse = jnp.log(lax.optimization_barrier(jnp.sum(jnp.exp(scores), axis=-1)))
    identity = jnp.eye(N_DP * B_DEV, dtype=jnp.float32)
    positive = lax.optimization_barrier(jnp.sum(scores * identity, axis=-1))
    losses = by_batch((lse - positive)[..., None]).reshape(N_DP, N_TABLE * B_DEV)
    dscore = (jnp.exp(scores - lse[..., None]) - identity).astype(jnp.bfloat16)
    dscore = lax.optimization_barrier(dscore).astype(jnp.float32)
    d_query = INVERSE_TEMP * jnp.einsum('tij,tjk->tik', dscore, keys)
    d_key = INVERSE_TEMP * jnp.einsum('tij,tik->tjk', dscore, queries)
    user_dout, user_dhid, user_dpool = tower_back(by_batch(d_query), user_output, user_pre, user_layer, user_head)
    item_dout, item_dhid, item_dpool = tower_back(by_batch(d_key), item_output, item_pre, item_layer, item_head)
    device_count = N_DP * N_TABLE

    def per_device(values):
        return values.reshape(device_count, B_DEV, values.shape[-1])

    def add_device(running, blocks):
        u_in, u_hid, u_dout, u_dhid, i_in, i_hid, i_dout, i_dhid = blocks
        terms = (rounded_term(u_in, u_dhid), rounded_term(u_hid, u_dout), rounded_term(i_in, i_dhid), rounded_term(i_hid, i_dout))
        return (tuple((a + b for a, b in zip(running, terms))), None)
    starts = (jnp.zeros(user_layer.shape, jnp.float32), jnp.zeros(user_head.shape, jnp.float32), jnp.zeros(item_layer.shape, jnp.float32), jnp.zeros(item_head.shape, jnp.float32))
    blocks = tuple((per_device(v) for v in (user_in, user_hidden, user_dout, user_dhid, item_in, item_hidden, item_dout, item_dhid)))
    changes, _ = lax.scan(add_device, starts, blocks)
    d_pooled = jnp.concatenate([user_dpool, item_dpool], axis=1).reshape(N_DP, group_rows, feature_count, EMB)

    def shard_grad(shard):
        shard_ids, shard_mults = shard_inputs(shard)

        def block_grad(triple):
            values = triple[2].astype(jnp.float32)[:, :, None, :] * triple[1].astype(jnp.float32)[..., None]
            return jax.ops.segment_sum(values.reshape(-1, EMB), triple[0].reshape(-1), num_segments=R_DEV)
        return lax.optimization_barrier(jnp.sum(lax.map(block_grad, (shard_ids, shard_mults, d_pooled)), axis=0))
    table_change = lax.map(shard_grad, shard_list).reshape(N_TABLE * R_DEV, EMB)
    return (losses, table_change, changes[0], changes[1], changes[2], changes[3])
```

```python
import functools

import jax
import jax.numpy as jnp
from jax import lax
from jax.experimental import pallas as pl
from jax.experimental.pallas import tpu as pltpu
from jax.sharding import PartitionSpec as P

LOOKUPS = 8


INVERSE_TEMP = 20.0
EPSILON = 1e-06


def silu_slope(pre):
    gate = jax.nn.sigmoid(pre)
    return gate * (1.0 + pre * (1.0 - gate))


def run_tower(pooled_in, layer, head):
    pre = jnp.dot(pooled_in, layer, preferred_element_type=jnp.float32)
    hidden = jax.nn.silu(pre).astype(jnp.bfloat16)
    output = jnp.dot(hidden, head, preferred_element_type=jnp.float32)
    scale = lax.rsqrt(jnp.sum(output * output, axis=-1, keepdims=True) + EPSILON)
    return (pre, hidden, output * scale, scale)


def tower_back(d_unit, unit, scale, pre, hidden, pooled_in, head):
    along = jnp.sum(unit * d_unit, axis=-1, keepdims=True)
    d_output = ((d_unit - unit * along) * scale).astype(jnp.bfloat16)
    back = lax.dot_general(
        d_output, head, (((1,), (1,)), ((), ())), preferred_element_type=jnp.float32
    )
    d_hidden = (back * silu_slope(pre)).astype(jnp.bfloat16)
    layer_term = lax.dot_general(
        pooled_in, d_hidden, (((0,), (0,)), ((), ())), preferred_element_type=jnp.float32
    )
    head_term = lax.dot_general(
        hidden, d_output, (((0,), (0,)), ((), ())), preferred_element_type=jnp.float32
    )
    return (d_output, d_hidden, layer_term, head_term)


def input_grads(d_hidden, layer):
    return lax.dot_general(
        d_hidden, layer, (((1,), (1,)), ((), ())), preferred_element_type=jnp.float32
    ).astype(jnp.bfloat16)


def shards_general(ids, mults, table, user_layer, user_head, item_layer, item_head, counts):
    table_count = lax.axis_size("table")
    rows_dev, emb_width = table.shape
    group_rows = ids.shape[1]
    feature_count = ids.shape[2] // LOOKUPS
    own_rows = group_rows // table_count
    user_width = user_layer.shape[0]
    id_blocks = ids[0].reshape(group_rows, feature_count, LOOKUPS).transpose(1, 0, 2)
    mult_blocks = mults[0].reshape(group_rows, feature_count, LOOKUPS).transpose(1, 0, 2)
    table_rows = lax.broadcasted_iota(jnp.int32, (1, rows_dev), 1)

    def lookup_weights(id_block, mult_block):
        running = jnp.zeros((group_rows, rows_dev), jnp.float32)
        for lookup in range(LOOKUPS):
            hit = id_block[:, lookup : lookup + 1] == table_rows
            running = running + jnp.where(
                hit, mult_block[:, lookup : lookup + 1].astype(jnp.float32), 0.0
            )
        return running.astype(jnp.bfloat16)

    def pool_feature(lookup_pair):
        weights = lookup_weights(lookup_pair[0], lookup_pair[1])
        return jnp.dot(weights, table, preferred_element_type=jnp.float32).astype(jnp.bfloat16)

    partial_value = lax.map(pool_feature, (id_blocks, mult_blocks))
    received = lax.all_to_all(partial_value, "table", split_axis=1, concat_axis=1, tiled=True)
    pooled = jnp.sum(
        received.astype(jnp.float32).reshape(feature_count, table_count, own_rows, emb_width),
        axis=1,
    ).astype(jnp.bfloat16)
    pooled = pooled.transpose(1, 0, 2).reshape(own_rows, feature_count * emb_width)
    user_in = pooled[:, :user_width]
    item_in = pooled[:, user_width:]
    user_pre, user_hidden, user_unit, user_scale = run_tower(user_in, user_layer, user_head)
    item_pre, item_hidden, item_unit, item_scale = run_tower(item_in, item_layer, item_head)
    user_vector = user_unit.astype(jnp.bfloat16)
    item_vector = item_unit.astype(jnp.bfloat16)
    item_rows, item_counts = (
        lax.all_gather(item_vector, "dp", axis=0, tiled=True),
        lax.all_gather(counts[0].astype(jnp.bfloat16), "dp", axis=0, tiled=True),
    )
    log_freq = jnp.log(item_counts.astype(jnp.float32))
    scores = (
        INVERSE_TEMP
        * lax.dot_general(
            user_vector, item_rows, (((1,), (1,)), ((), ())), preferred_element_type=jnp.float32
        )
        - log_freq[None, :]
    )
    lse = jnp.log(jnp.sum(jnp.exp(scores), axis=-1))
    own_index = lax.axis_index("dp") * own_rows + lax.broadcasted_iota(jnp.int32, (own_rows,), 0)
    columns = lax.broadcasted_iota(jnp.int32, scores.shape, 1)
    is_positive = columns == own_index[:, None]
    positive = jnp.sum(jnp.where(is_positive, scores, 0.0), axis=-1)
    losses = (lse - positive)[None, :]
    dscore = (jnp.exp(scores - lse[:, None]) - is_positive.astype(jnp.float32)).astype(jnp.bfloat16)
    d_user = INVERSE_TEMP * jnp.dot(dscore, item_rows, preferred_element_type=jnp.float32)
    item_terms = INVERSE_TEMP * lax.dot_general(
        dscore, user_vector, (((0,), (0,)), ((), ())), preferred_element_type=jnp.float32
    )
    d_item = lax.psum_scatter(
        item_terms.astype(jnp.bfloat16), "dp", scatter_dimension=0, tiled=True
    ).astype(jnp.float32)
    user_dout, user_dhid, user_layer_term, user_head_term = tower_back(
        d_user, user_unit, user_scale, user_pre, user_hidden, user_in, user_head
    )
    item_dout, item_dhid, item_layer_term, item_head_term = tower_back(
        d_item, item_unit, item_scale, item_pre, item_hidden, item_in, item_head
    )
    own_grads = jnp.concatenate(
        [input_grads(user_dhid, user_layer), input_grads(item_dhid, item_layer)], axis=1
    )
    group_grads = lax.all_gather(own_grads, "table", axis=0, tiled=True)

    def add_feature(feature, running):
        weights = lookup_weights(id_blocks[feature], mult_blocks[feature])
        column = lax.dynamic_slice_in_dim(group_grads, feature * emb_width, emb_width, 1)
        return running + lax.dot_general(
            weights, column, (((0,), (0,)), ((), ())), preferred_element_type=jnp.float32
        )

    table_part = lax.fori_loop(
        0, feature_count, add_feature, jnp.zeros((rows_dev, emb_width), jnp.float32)
    )
    layer_rows = (
        lax.psum_scatter(
            user_layer_term.astype(jnp.bfloat16), "table", scatter_dimension=0, tiled=True
        ).astype(jnp.float32),
        lax.psum_scatter(
            user_head_term.astype(jnp.bfloat16), "table", scatter_dimension=0, tiled=True
        ).astype(jnp.float32),
        lax.psum_scatter(
            item_layer_term.astype(jnp.bfloat16), "table", scatter_dimension=0, tiled=True
        ).astype(jnp.float32),
        lax.psum_scatter(
            item_head_term.astype(jnp.bfloat16), "table", scatter_dimension=0, tiled=True
        ).astype(jnp.float32),
    )
    totals = (
        lax.psum(table_part.astype(jnp.bfloat16), "dp").astype(jnp.float32),
        lax.psum(layer_rows[0].astype(jnp.bfloat16), "dp").astype(jnp.float32),
        lax.psum(layer_rows[1].astype(jnp.bfloat16), "dp").astype(jnp.float32),
        lax.psum(layer_rows[2].astype(jnp.bfloat16), "dp").astype(jnp.float32),
        lax.psum(layer_rows[3].astype(jnp.bfloat16), "dp").astype(jnp.float32),
    )
    return (losses, totals[0], totals[1], totals[2], totals[3], totals[4])


BF16 = jnp.bfloat16
F32 = jnp.float32
ROW_ID = jnp.int16
CHUNKS = 4
MESH = pl.DeviceIdType.MESH


def flip(value, mask, bits):
    out = 0
    for bit in range(bits):
        one = lax.rem(lax.div(value, 1 << bit), 2)
        if (mask >> bit) & 1:
            one = 1 - one
        out = out + one * (1 << bit)
    return out


def dot_nt(left, right):
    return lax.dot_general(left, right, (((1,), (1,)), ((), ())), preferred_element_type=F32)


def dot_tn(left, right):
    return lax.dot_general(left, right, (((0,), (0,)), ((), ())), preferred_element_type=F32)


def step_kernel(
    ids_ref,
    mults_ref,
    table_ref,
    user_layer_ref,
    user_head_ref,
    item_layer_ref,
    item_head_ref,
    counts_ref,
    losses_ref,
    table_out,
    user_layer_out,
    user_head_out,
    item_layer_out,
    item_head_out,
    ids_t,
    mults_t,
    table_t,
    row_ids,
    weights,
    parts,
    pair_in,
    sums,
    sums_in,
    slices,
    slices_in,
    units,
    grads,
    tower_terms,
    tower_in,
    tower_all,
    table_terms,
    table_in,
    table_all,
    pair_sems,
    sums_sems,
    slices_sems,
    units_sems,
    grads_sems,
    pass_sems,
    tower_sems,
    tower_all_sems,
    table_sems,
    table_all_sems,
):
    t = lax.axis_index("table")
    d = lax.axis_index("dp")
    z = lax.div(t, 2)
    core = lax.rem(t, 2)
    sibling = z * 2 + (1 - core)
    z_peers = [flip(z, k, 2) for k in range(4)]
    dp_peers = [flip(d, k, 2) for k in range(4)]

    barrier = pltpu.get_barrier_semaphore()
    for k in range(1, 8):
        pl.semaphore_signal(barrier, inc=1, device_id={"table": flip(t, k, 3)}, device_id_type=MESH)
    for k in range(1, 4):
        pl.semaphore_signal(barrier, inc=1, device_id={"dp": dp_peers[k]}, device_id_type=MESH)

    def send(src, dst, sems, index, target):
        copy = pltpu.make_async_remote_copy(
            src_ref=src,
            dst_ref=dst,
            send_sem=sems.at[0, index],
            recv_sem=sems.at[1, index],
            device_id=target,
            device_id_type=MESH,
        )
        copy.start()
        return copy

    ids_t[...] = ids_ref[...].T
    mults_t[...] = mults_ref[...].T
    table_t[...] = table_ref[...].T
    row_ids[...] = lax.broadcasted_iota(jnp.int32, row_ids.shape, 0).astype(row_ids.dtype)
    block = 128

    def pool_pair(chunk, pair):
        for half in range(2):
            feature = chunk * 4 + pair * 2 + half
            slots = pl.ds(pl.multiple_of(feature * 8, 8), 8)
            id_rows = ids_t[slots, :]
            mult_rows = mults_t[slots, :].astype(F32)
            spread = [
                (
                    jnp.broadcast_to(id_rows[l : l + 1, :], (16, 128)).astype(row_ids.dtype),
                    jnp.broadcast_to(mult_rows[l : l + 1, :], (16, 128)).astype(BF16),
                )
                for l in range(LOOKUPS)
            ]
            lanes = pl.ds(pl.multiple_of(feature * 128, 128), 128)
            for start in range(0, 1024, block):
                here = row_ids[start : start + block, :].reshape(block // 16, 16, 128)
                total = None
                for id_row, mult_row in spread:
                    term = jnp.where(here == id_row[None], mult_row[None], jnp.zeros((), BF16))
                    total = term if total is None else total + term
                weights[start : start + block, lanes] = total.reshape(block, 128)
        lanes = pl.ds(pl.multiple_of((chunk * 4 + pair * 2) * 128, 256), 256)
        pooled_t = jnp.dot(table_t[...], weights[:, lanes], preferred_element_type=F32)
        for half in range(2):
            pooled = pooled_t[:, half * 128 : half * 128 + 128].T.astype(BF16)
            place = pl.ds(pl.multiple_of((pair * 2 + half) * 128, 128), 128)
            for owner in range(8):
                parts[chunk, owner % 2, owner // 2, :, place] = pooled[owner * 16 : owner * 16 + 16]

    pair_copies, sums_copies = [], []

    def pass_on(chunk):
        pair_copies[chunk].wait_recv()
        total = parts[chunk, core].astype(F32) + pair_in[chunk].astype(F32)
        sums[chunk] = total.astype(BF16)
        for k in range(1, 4):
            sums_copies.append(
                send(
                    sums.at[chunk, z_peers[k]],
                    sums_in.at[chunk, k - 1],
                    sums_sems,
                    chunk * 3 + k - 1,
                    {"table": z_peers[k] * 2 + core},
                )
            )

    for chunk in range(CHUNKS):

        def pool_step(pair, carry):
            pool_pair(chunk, pair)
            return carry

        lax.fori_loop(0, 2, pool_step, 0)
        if chunk == 0:
            pl.semaphore_wait(barrier, 10)
        pair_copies.append(
            send(
                parts.at[chunk, 1 - core],
                pair_in.at[chunk],
                pair_sems,
                chunk,
                {"table": sibling},
            )
        )
        if chunk > 0:
            pass_on(chunk - 1)
    pass_on(CHUNKS - 1)
    pooled = []
    for chunk in range(CHUNKS):
        total = sums[chunk, z].astype(F32)
        for k in range(3):
            sums_copies[chunk * 3 + k].wait_recv()
            total = total + sums_in[chunk, k].astype(F32)
        pooled.append(total.astype(BF16))
    user_in = jnp.concatenate(pooled[:2], axis=1)
    item_in = jnp.concatenate(pooled[2:], axis=1)

    user_pre, user_hidden, user_unit, user_scale = run_tower(
        user_in, user_layer_ref[...], user_head_ref[...]
    )
    item_pre, item_hidden, item_unit, item_scale = run_tower(
        item_in, item_layer_ref[...], item_head_ref[...]
    )
    eye16 = lax.broadcasted_iota(jnp.int32, (16, 16), 0) == lax.broadcasted_iota(
        jnp.int32, (16, 16), 1
    )
    count_column = jnp.sum(
        jnp.where(eye16, jnp.broadcast_to(counts_ref[...].astype(F32), (16, 16)), 0.0),
        axis=1,
        keepdims=True,
    )
    units[0, :, 0:128] = user_unit.astype(BF16)
    units[0, :, 128:256] = item_unit.astype(BF16)
    units[0, :, 256:384] = jnp.broadcast_to(count_column, (16, 128)).astype(BF16)
    units_copies = [
        send(units.at[0], units.at[k], units_sems, k - 1, {"dp": dp_peers[k]}) for k in range(1, 4)
    ]
    for owner in range(8):
        slices[owner, :, 0:128] = user_in[:, owner * 128 : owner * 128 + 128]
        slices[owner, :, 128:256] = item_in[:, owner * 128 : owner * 128 + 128]
        slices[owner, :, 256:384] = jnp.concatenate(
            [
                user_hidden[:, owner * 64 : owner * 64 + 64],
                item_hidden[:, owner * 64 : owner * 64 + 64],
            ],
            axis=1,
        )
    slices_copies = []
    for k in range(1, 8):
        peer = flip(t, k, 3)
        slices_copies.append(
            send(slices.at[peer], slices_in.at[t], slices_sems, k - 1, {"table": peer})
        )
    slices_in[t] = slices[t]
    for copy in units_copies:
        copy.wait_recv()

    every = units[...]
    users = every[:, :, 0:128].reshape(64, 128)
    items = every[:, :, 128:256].reshape(64, 128)
    log_freq = jnp.log(every[:, :, 256:384].reshape(64, 128).astype(F32))[:, 0:1]
    scores = INVERSE_TEMP * dot_nt(items, users) - log_freq
    lse = jnp.log(jnp.sum(jnp.exp(scores), axis=0, keepdims=True))
    same = lax.broadcasted_iota(jnp.int32, (64, 64), 0) == lax.broadcasted_iota(
        jnp.int32, (64, 64), 1
    )
    positive = jnp.sum(jnp.where(same, scores, 0.0), axis=0, keepdims=True)
    losses_ref[...] = (lse - positive)[:, 0:16]
    dscore = (jnp.exp(scores - lse) - jnp.where(same, 1.0, 0.0)).astype(BF16)
    d_user = INVERSE_TEMP * dot_tn(dscore, items)[0:16]
    d_item = INVERSE_TEMP * jnp.dot(dscore[0:16], users, preferred_element_type=F32)

    def back(d_unit, unit, scale, pre, head_ref):
        along = jnp.sum(unit * d_unit, axis=-1, keepdims=True)
        d_output = ((d_unit - unit * along) * scale).astype(BF16)
        d_hidden = (dot_nt(d_output, head_ref[...]) * silu_slope(pre)).astype(BF16)
        return d_output, d_hidden

    user_dout, user_dhid = back(d_user, user_unit, user_scale, user_pre, user_head_ref)
    item_dout, item_dhid = back(d_item, item_unit, item_scale, item_pre, item_head_ref)
    grads[t] = jnp.concatenate([user_dhid, item_dhid, user_dout, item_dout], axis=1)
    grads_copies = [
        send(
            grads.at[t], grads.at[t], grads_sems, k - 1, {"table": z_peers[k] * 2 + core}
        )
        for k in range(1, 4)
    ]
    pass_copies = [send(grads.at[t], grads.at[t], pass_sems, 0, {"table": sibling})]
    for k in range(1, 4):
        grads_copies[k - 1].wait_recv()
        slot = z_peers[k] * 2 + core
        pass_copies.append(
            send(grads.at[slot], grads.at[slot], pass_sems, k, {"table": sibling})
        )
    for copy in pass_copies:
        copy.wait_recv()
    for copy in slices_copies:
        copy.wait_recv()

    every = grads[...].reshape(128, 1280)
    kept = slices_in[...].reshape(128, 384)
    user_rows = dot_tn(kept[:, 0:128], every[:, 0:512]).astype(BF16)
    item_rows = dot_tn(kept[:, 128:256], every[:, 512:1024]).astype(BF16)
    head_rows = dot_tn(kept[:, 256:384], every[:, 1024:1280]).astype(BF16)
    for part in range(4):
        lanes = slice(part * 128, part * 128 + 128)
        tower_terms[part, 0:128, :] = user_rows[:, lanes]
        tower_terms[part, 128:256, :] = item_rows[:, lanes]
        tower_terms[part, 256:272, :] = head_rows[part * 16 : part * 16 + 16, 0:128]
        tower_terms[part, 272:288, :] = head_rows[64 + part * 16 : 80 + part * 16, 128:256]
    tower_copies = [
        send(
            tower_terms.at[dp_peers[k]], tower_in.at[k - 1], tower_sems, k - 1, {"dp": dp_peers[k]}
        )
        for k in range(1, 4)
    ]

    user_dpool = dot_nt(every[:, 0:512], user_layer_ref[...]).astype(BF16)
    item_dpool = dot_nt(every[:, 512:1024], item_layer_ref[...]).astype(BF16)
    columns = [user_dpool[:, f * 128 : f * 128 + 128] for f in range(8)] + [
        item_dpool[:, f * 128 : f * 128 + 128] for f in range(8)
    ]
    d_pooled = jnp.concatenate(columns, axis=0)
    for part in range(4):
        table_terms[part] = jnp.dot(
            weights[part * 256 : part * 256 + 256, :], d_pooled, preferred_element_type=F32
        ).astype(BF16)
    table_copies = [
        send(
            table_terms.at[dp_peers[k]], table_in.at[k - 1], table_sems, k - 1, {"dp": dp_peers[k]}
        )
        for k in range(1, 4)
    ]

    def gather_sum(terms, arrived, copies, result, sems):
        total = terms[d].astype(F32)
        for k in range(3):
            copies[k].wait_recv()
            total = total + arrived[k].astype(F32)
        result[d] = total.astype(BF16)
        return [
            send(result.at[d], result.at[d], sems, k - 1, {"dp": dp_peers[k]}) for k in range(1, 4)
        ]

    tower_all_copies = gather_sum(tower_terms, tower_in, tower_copies, tower_all, tower_all_sems)
    table_all_copies = gather_sum(table_terms, table_in, table_copies, table_all, table_all_sems)
    for copy in tower_all_copies:
        copy.wait_recv()
    for part in range(4):
        lanes = slice(part * 128, part * 128 + 128)
        rows = slice(part * 16, part * 16 + 16)
        user_layer_out[:, lanes] = tower_all[part, 0:128, :].astype(F32)
        item_layer_out[:, lanes] = tower_all[part, 128:256, :].astype(F32)
        user_head_out[rows, :] = tower_all[part, 256:272, :].astype(F32)
        item_head_out[rows, :] = tower_all[part, 272:288, :].astype(F32)
    for copy in table_all_copies:
        copy.wait_recv()
    for part in range(4):
        table_out[part * 256 : part * 256 + 256, :] = table_all[part].astype(F32)
    for copy in (
        pair_copies
        + sums_copies
        + units_copies
        + slices_copies
        + grads_copies
        + pass_copies
        + tower_copies
        + table_copies
        + tower_all_copies
        + table_all_copies
    ):
        copy.wait_send()


def shards(ids, mults, table, user_layer, user_head, item_layer, item_head, counts):
    small = lax.axis_size("table") == 8 and lax.axis_size("dp") == 4
    if not small or ids.shape != (1, 128, 128) or table.shape != (1024, 128):
        return shards_general(
            ids, mults, table, user_layer, user_head, item_layer, item_head, counts
        )

    def dma(count):
        return pltpu.SemaphoreType.DMA((2, count))

    vmem = pl.BlockSpec(memory_space=pltpu.VMEM)
    return pl.pallas_call(
        step_kernel,
        out_shape=(
            jax.ShapeDtypeStruct((1, 16), F32),
            jax.ShapeDtypeStruct((1024, 128), F32),
            jax.ShapeDtypeStruct((128, 512), F32),
            jax.ShapeDtypeStruct((64, 128), F32),
            jax.ShapeDtypeStruct((128, 512), F32),
            jax.ShapeDtypeStruct((64, 128), F32),
        ),
        in_specs=[vmem] * 8,
        out_specs=(vmem,) * 6,
        scratch_shapes=[
            pltpu.VMEM((128, 128), jnp.int32),
            pltpu.VMEM((128, 128), jnp.int32),
            pltpu.VMEM((128, 1024), BF16),
            pltpu.VMEM((1024, 128), ROW_ID),
            pltpu.VMEM((1024, 2048), BF16),
            pltpu.VMEM((CHUNKS, 2, 4, 16, 512), BF16),
            pltpu.VMEM((CHUNKS, 4, 16, 512), BF16),
            pltpu.VMEM((CHUNKS, 4, 16, 512), BF16),
            pltpu.VMEM((CHUNKS, 3, 16, 512), BF16),
            pltpu.VMEM((8, 16, 384), BF16),
            pltpu.VMEM((8, 16, 384), BF16),
            pltpu.VMEM((4, 16, 384), BF16),
            pltpu.VMEM((8, 16, 1280), BF16),
            pltpu.VMEM((4, 288, 128), BF16),
            pltpu.VMEM((3, 288, 128), BF16),
            pltpu.VMEM((4, 288, 128), BF16),
            pltpu.VMEM((4, 256, 128), BF16),
            pltpu.VMEM((3, 256, 128), BF16),
            pltpu.VMEM((4, 256, 128), BF16),
            dma(CHUNKS),
            dma(CHUNKS * 3),
            dma(7),
            dma(3),
            dma(3),
            dma(4),
            dma(3),
            dma(3),
            dma(3),
            dma(3),
        ],
        compiler_params=pltpu.CompilerParams(
            collective_id=0, has_side_effects=True, vmem_limit_bytes=40 * 1024 * 1024
        ),
        cost_estimate=pl.CostEstimate(
            flops=3_000_000_000, bytes_accessed=4_500_000, transcendentals=100_000
        ),
    )(ids[0], mults[0], table, user_layer, user_head, item_layer, item_head, counts)


def solution(mesh):
    in_specs = (
        P("table", "dp", None),
        P("table", "dp", None),
        P("table", None),
        P(),
        P(),
        P(),
        P(),
        P("dp", "table"),
    )
    out_specs = (
        P("dp", "table"),
        P("table", None),
        P("table", None),
        P("table", None),
        P("table", None),
        P("table", None),
    )
    return jax.shard_map(shards, mesh=mesh, in_specs=in_specs, out_specs=out_specs, check_vma=False)
```

```python
import functools

import jax
import jax.numpy as jnp
from jax import lax
from jax.experimental import pallas as pl
from jax.experimental.pallas import tpu as pltpu
from jax.sharding import PartitionSpec as P

LOOKUPS = 8


INVERSE_TEMP = 20.0
EPSILON = 1e-06


def silu_slope(pre):
    gate = jax.nn.sigmoid(pre)
    return gate * (1.0 + pre * (1.0 - gate))


def run_tower(pooled_in, layer, head):
    pre = jnp.dot(pooled_in, layer, preferred_element_type=jnp.float32)
    hidden = jax.nn.silu(pre).astype(jnp.bfloat16)
    output = jnp.dot(hidden, head, preferred_element_type=jnp.float32)
    scale = lax.rsqrt(jnp.sum(output * output, axis=-1, keepdims=True) + EPSILON)
    return (pre, hidden, output * scale, scale)


def tower_back(d_unit, unit, scale, pre, hidden, pooled_in, head):
    along = jnp.sum(unit * d_unit, axis=-1, keepdims=True)
    d_output = ((d_unit - unit * along) * scale).astype(jnp.bfloat16)
    back = lax.dot_general(
        d_output, head, (((1,), (1,)), ((), ())), preferred_element_type=jnp.float32
    )
    d_hidden = (back * silu_slope(pre)).astype(jnp.bfloat16)
    layer_term = lax.dot_general(
        pooled_in, d_hidden, (((0,), (0,)), ((), ())), preferred_element_type=jnp.float32
    )
    head_term = lax.dot_general(
        hidden, d_output, (((0,), (0,)), ((), ())), preferred_element_type=jnp.float32
    )
    return (d_output, d_hidden, layer_term, head_term)


def input_grads(d_hidden, layer):
    return lax.dot_general(
        d_hidden, layer, (((1,), (1,)), ((), ())), preferred_element_type=jnp.float32
    ).astype(jnp.bfloat16)


def shards_general(ids, mults, table, user_layer, user_head, item_layer, item_head, counts):
    table_count = lax.axis_size("table")
    rows_dev, emb_width = table.shape
    group_rows = ids.shape[1]
    feature_count = ids.shape[2] // LOOKUPS
    own_rows = group_rows // table_count
    user_width = user_layer.shape[0]
    id_blocks = ids[0].reshape(group_rows, feature_count, LOOKUPS).transpose(1, 0, 2)
    mult_blocks = mults[0].reshape(group_rows, feature_count, LOOKUPS).transpose(1, 0, 2)
    table_rows = lax.broadcasted_iota(jnp.int32, (1, rows_dev), 1)

    def lookup_weights(id_block, mult_block):
        running = jnp.zeros((group_rows, rows_dev), jnp.float32)
        for lookup in range(LOOKUPS):
            hit = id_block[:, lookup : lookup + 1] == table_rows
            running = running + jnp.where(
                hit, mult_block[:, lookup : lookup + 1].astype(jnp.float32), 0.0
            )
        return running.astype(jnp.bfloat16)

    def pool_feature(lookup_pair):
        weights = lookup_weights(lookup_pair[0], lookup_pair[1])
        return jnp.dot(weights, table, preferred_element_type=jnp.float32).astype(jnp.bfloat16)

    partial_value = lax.map(pool_feature, (id_blocks, mult_blocks))
    received = lax.all_to_all(partial_value, "table", split_axis=1, concat_axis=1, tiled=True)
    pooled = jnp.sum(
        received.astype(jnp.float32).reshape(feature_count, table_count, own_rows, emb_width),
        axis=1,
    ).astype(jnp.bfloat16)
    pooled = pooled.transpose(1, 0, 2).reshape(own_rows, feature_count * emb_width)
    user_in = pooled[:, :user_width]
    item_in = pooled[:, user_width:]
    user_pre, user_hidden, user_unit, user_scale = run_tower(user_in, user_layer, user_head)
    item_pre, item_hidden, item_unit, item_scale = run_tower(item_in, item_layer, item_head)
    user_vector = user_unit.astype(jnp.bfloat16)
    item_vector = item_unit.astype(jnp.bfloat16)
    item_rows, item_counts = (
        lax.all_gather(item_vector, "dp", axis=0, tiled=True),
        lax.all_gather(counts[0].astype(jnp.bfloat16), "dp", axis=0, tiled=True),
    )
    log_freq = jnp.log(item_counts.astype(jnp.float32))
    scores = (
        INVERSE_TEMP
        * lax.dot_general(
            user_vector, item_rows, (((1,), (1,)), ((), ())), preferred_element_type=jnp.float32
        )
        - log_freq[None, :]
    )
    lse = jnp.log(jnp.sum(jnp.exp(scores), axis=-1))
    own_index = lax.axis_index("dp") * own_rows + lax.broadcasted_iota(jnp.int32, (own_rows,), 0)
    columns = lax.broadcasted_iota(jnp.int32, scores.shape, 1)
    is_positive = columns == own_index[:, None]
    positive = jnp.sum(jnp.where(is_positive, scores, 0.0), axis=-1)
    losses = (lse - positive)[None, :]
    dscore = (jnp.exp(scores - lse[:, None]) - is_positive.astype(jnp.float32)).astype(jnp.bfloat16)
    d_user = INVERSE_TEMP * jnp.dot(dscore, item_rows, preferred_element_type=jnp.float32)
    item_terms = INVERSE_TEMP * lax.dot_general(
        dscore, user_vector, (((0,), (0,)), ((), ())), preferred_element_type=jnp.float32
    )
    d_item = lax.psum_scatter(
        item_terms.astype(jnp.bfloat16), "dp", scatter_dimension=0, tiled=True
    ).astype(jnp.float32)
    user_dout, user_dhid, user_layer_term, user_head_term = tower_back(
        d_user, user_unit, user_scale, user_pre, user_hidden, user_in, user_head
    )
    item_dout, item_dhid, item_layer_term, item_head_term = tower_back(
        d_item, item_unit, item_scale, item_pre, item_hidden, item_in, item_head
    )
    own_grads = jnp.concatenate(
        [input_grads(user_dhid, user_layer), input_grads(item_dhid, item_layer)], axis=1
    )
    group_grads = lax.all_gather(own_grads, "table", axis=0, tiled=True)

    def add_feature(feature, running):
        weights = lookup_weights(id_blocks[feature], mult_blocks[feature])
        column = lax.dynamic_slice_in_dim(group_grads, feature * emb_width, emb_width, 1)
        return running + lax.dot_general(
            weights, column, (((0,), (0,)), ((), ())), preferred_element_type=jnp.float32
        )

    table_part = lax.fori_loop(
        0, feature_count, add_feature, jnp.zeros((rows_dev, emb_width), jnp.float32)
    )
    layer_rows = (
        lax.psum_scatter(
            user_layer_term.astype(jnp.bfloat16), "table", scatter_dimension=0, tiled=True
        ).astype(jnp.float32),
        lax.psum_scatter(
            user_head_term.astype(jnp.bfloat16), "table", scatter_dimension=0, tiled=True
        ).astype(jnp.float32),
        lax.psum_scatter(
            item_layer_term.astype(jnp.bfloat16), "table", scatter_dimension=0, tiled=True
        ).astype(jnp.float32),
        lax.psum_scatter(
            item_head_term.astype(jnp.bfloat16), "table", scatter_dimension=0, tiled=True
        ).astype(jnp.float32),
    )
    totals = (
        lax.psum(table_part.astype(jnp.bfloat16), "dp").astype(jnp.float32),
        lax.psum(layer_rows[0].astype(jnp.bfloat16), "dp").astype(jnp.float32),
        lax.psum(layer_rows[1].astype(jnp.bfloat16), "dp").astype(jnp.float32),
        lax.psum(layer_rows[2].astype(jnp.bfloat16), "dp").astype(jnp.float32),
        lax.psum(layer_rows[3].astype(jnp.bfloat16), "dp").astype(jnp.float32),
    )
    return (losses, totals[0], totals[1], totals[2], totals[3], totals[4])


BF16 = jnp.bfloat16
F32 = jnp.float32
ROW_ID = jnp.int16
CHUNKS = 4
MESH = pl.DeviceIdType.MESH


def flip(value, mask, bits):
    out = 0
    for bit in range(bits):
        one = lax.rem(lax.div(value, 1 << bit), 2)
        if (mask >> bit) & 1:
            one = 1 - one
        out = out + one * (1 << bit)
    return out


def dot_nt(left, right):
    return lax.dot_general(left, right, (((1,), (1,)), ((), ())), preferred_element_type=F32)


def dot_tn(left, right):
    return lax.dot_general(left, right, (((0,), (0,)), ((), ())), preferred_element_type=F32)


def step_kernel(
    ids_hbm,
    mults_hbm,
    table_hbm,
    user_layer_hbm,
    user_head_hbm,
    item_layer_hbm,
    item_head_hbm,
    counts_hbm,
    losses_ref,
    tower_all,
    table_all,
    ids_ref,
    mults_ref,
    table_ref,
    user_layer_ref,
    user_head_ref,
    item_layer_ref,
    item_head_ref,
    counts_ref,
    user_layer_t,
    user_head_t,
    item_layer_t,
    item_head_t,
    ids_t,
    mults_t,
    table_t,
    row_ids,
    weights,
    parts,
    pair_in,
    sums,
    sums_in,
    slices,
    slices_in,
    units,
    grads,
    tower_terms,
    tower_in,
    table_terms,
    table_in,
    load_sems,
    pair_sems,
    sums_sems,
    slices_sems,
    units_sems,
    grads_sems,
    pass_sems,
    tower_sems,
    tower_all_sems,
    table_sems,
    table_all_sems,
):
    pairs = (
        (ids_hbm, ids_ref),
        (mults_hbm, mults_ref),
        (table_hbm, table_ref),
        (user_layer_hbm, user_layer_ref),
        (item_layer_hbm, item_layer_ref),
        (user_head_hbm, user_head_ref),
        (item_head_hbm, item_head_ref),
        (counts_hbm, counts_ref),
    )
    loads = [pltpu.make_async_copy(a, b, load_sems.at[i]) for i, (a, b) in enumerate(pairs)]
    for load in loads:
        load.start()
    t = lax.axis_index("table")
    d = lax.axis_index("dp")
    z = lax.div(t, 2)
    core = lax.rem(t, 2)
    sibling = z * 2 + (1 - core)
    z_peers = [flip(z, k, 2) for k in range(4)]
    dp_peers = [flip(d, k, 2) for k in range(4)]

    barrier = pltpu.get_barrier_semaphore()
    for k in range(1, 8):
        pl.semaphore_signal(barrier, inc=1, device_id={"table": flip(t, k, 3)}, device_id_type=MESH)
    for k in range(1, 4):
        pl.semaphore_signal(barrier, inc=1, device_id={"dp": dp_peers[k]}, device_id_type=MESH)

    def send(src, dst, sems, index, target):
        copy = pltpu.make_async_remote_copy(
            src_ref=src,
            dst_ref=dst,
            send_sem=sems.at[0, index],
            recv_sem=sems.at[1, index],
            device_id=target,
            device_id_type=MESH,
        )
        copy.start()
        return copy

    row_ids[...] = lax.broadcasted_iota(jnp.int32, row_ids.shape, 0).astype(row_ids.dtype)
    for load in loads[:3]:
        load.wait()
    ids_t[...] = ids_ref[...].T
    mults_t[...] = mults_ref[...].T
    table_t[...] = table_ref[...].T
    block = 128

    def pool_pair(chunk, pair):
        for half in range(2):
            feature = chunk * 4 + pair * 2 + half
            slots = pl.ds(pl.multiple_of(feature * 8, 8), 8)
            id_rows = ids_t[slots, :]
            mult_rows = mults_t[slots, :].astype(F32)
            spread = [
                (
                    jnp.broadcast_to(id_rows[l : l + 1, :], (16, 128)).astype(row_ids.dtype),
                    jnp.broadcast_to(mult_rows[l : l + 1, :], (16, 128)).astype(BF16),
                )
                for l in range(LOOKUPS)
            ]
            lanes = pl.ds(pl.multiple_of(feature * 128, 128), 128)
            for start in range(0, 1024, block):
                here = row_ids[start : start + block, :].reshape(block // 16, 16, 128)
                total = None
                for id_row, mult_row in spread:
                    term = jnp.where(here == id_row[None], mult_row[None], jnp.zeros((), BF16))
                    total = term if total is None else total + term
                weights[start : start + block, lanes] = total.reshape(block, 128)
        lanes = pl.ds(pl.multiple_of((chunk * 4 + pair * 2) * 128, 256), 256)
        pooled_t = jnp.dot(table_t[...], weights[:, lanes], preferred_element_type=F32)
        for half in range(2):
            pooled = pooled_t[:, half * 128 : half * 128 + 128].T.astype(BF16)
            place = pl.ds(pl.multiple_of((pair * 2 + half) * 128, 128), 128)
            for owner in range(8):
                parts[chunk, owner % 2, owner // 2, :, place] = pooled[owner * 16 : owner * 16 + 16]

    pair_copies, sums_copies = [], []

    def pass_on(chunk):
        pair_copies[chunk].wait_recv()
        total = parts[chunk, core].astype(F32) + pair_in[chunk].astype(F32)
        sums[chunk] = total.astype(BF16)
        for k in range(1, 4):
            sums_copies.append(
                send(
                    sums.at[chunk, z_peers[k]],
                    sums_in.at[chunk, k - 1],
                    sums_sems,
                    chunk * 3 + k - 1,
                    {"table": z_peers[k] * 2 + core},
                )
            )

    for chunk in range(CHUNKS):

        def pool_step(pair, carry):
            pool_pair(chunk, pair)
            return carry

        lax.fori_loop(0, 2, pool_step, 0)
        if chunk == 0:
            pl.semaphore_wait(barrier, 10)
        pair_copies.append(
            send(
                parts.at[chunk, 1 - core],
                pair_in.at[chunk],
                pair_sems,
                chunk,
                {"table": sibling},
            )
        )
        if chunk > 0:
            pass_on(chunk - 1)
    for load in loads[3:]:
        load.wait()
    pass_on(CHUNKS - 1)
    user_head_t[...] = user_head_ref[...].T
    item_head_t[...] = item_head_ref[...].T
    pooled = []
    for chunk in range(CHUNKS):
        total = sums[chunk, z].astype(F32)
        for k in range(3):
            sums_copies[chunk * 3 + k].wait_recv()
            total = total + sums_in[chunk, k].astype(F32)
        pooled.append(total.astype(BF16))
    user_in = jnp.concatenate(pooled[:2], axis=1)
    item_in = jnp.concatenate(pooled[2:], axis=1)

    user_pre, user_hidden, user_unit, user_scale = run_tower(
        user_in, user_layer_ref[...], user_head_ref[...]
    )
    item_pre, item_hidden, item_unit, item_scale = run_tower(
        item_in, item_layer_ref[...], item_head_ref[...]
    )
    eye16 = lax.broadcasted_iota(jnp.int32, (16, 16), 0) == lax.broadcasted_iota(
        jnp.int32, (16, 16), 1
    )
    count_column = jnp.sum(
        jnp.where(eye16, jnp.broadcast_to(counts_ref[...].astype(F32), (16, 16)), 0.0),
        axis=1,
        keepdims=True,
    )
    units[0, :, 0:128] = user_unit.astype(BF16)
    units[0, :, 128:256] = item_unit.astype(BF16)
    units[0, :, 256:384] = jnp.broadcast_to(count_column, (16, 128)).astype(BF16)
    units_copies = [
        send(units.at[0], units.at[k], units_sems, k - 1, {"dp": dp_peers[k]}) for k in range(1, 4)
    ]
    for owner in range(8):
        slices[owner, :, 0:128] = user_in[:, owner * 128 : owner * 128 + 128]
        slices[owner, :, 128:256] = item_in[:, owner * 128 : owner * 128 + 128]
        slices[owner, :, 256:384] = jnp.concatenate(
            [
                user_hidden[:, owner * 64 : owner * 64 + 64],
                item_hidden[:, owner * 64 : owner * 64 + 64],
            ],
            axis=1,
        )
    slices_copies = []
    for k in range(1, 8):
        peer = flip(t, k, 3)
        slices_copies.append(
            send(slices.at[peer], slices_in.at[t], slices_sems, k - 1, {"table": peer})
        )
    slices_in[t] = slices[t]
    for copy in units_copies:
        copy.wait_recv()

    every = units[...]
    users = every[:, :, 0:128].reshape(64, 128)
    items = every[:, :, 128:256].reshape(64, 128)
    log_freq = jnp.log(every[:, :, 256:384].reshape(64, 128).astype(F32))[:, 0:1]
    scores = INVERSE_TEMP * dot_nt(items, users) - log_freq
    lse = jnp.log(jnp.sum(jnp.exp(scores), axis=0, keepdims=True))
    same = lax.broadcasted_iota(jnp.int32, (64, 64), 0) == lax.broadcasted_iota(
        jnp.int32, (64, 64), 1
    )
    positive = jnp.sum(jnp.where(same, scores, 0.0), axis=0, keepdims=True)
    losses_ref[...] = (lse - positive)[:, 0:16]
    dscore = (jnp.exp(scores - lse) - jnp.where(same, 1.0, 0.0)).astype(BF16)
    d_user = INVERSE_TEMP * dot_tn(dscore, items)[0:16]
    d_item = INVERSE_TEMP * jnp.dot(dscore[0:16], users, preferred_element_type=F32)

    def back(d_unit, unit, scale, pre, head_t):
        along = jnp.sum(unit * d_unit, axis=-1, keepdims=True)
        d_output = ((d_unit - unit * along) * scale).astype(BF16)
        d_hidden = (
            jnp.dot(d_output, head_t[...], preferred_element_type=F32) * silu_slope(pre)
        ).astype(BF16)
        return d_output, d_hidden

    user_dout, user_dhid = back(d_user, user_unit, user_scale, user_pre, user_head_t)
    item_dout, item_dhid = back(d_item, item_unit, item_scale, item_pre, item_head_t)
    grads[t] = jnp.concatenate([user_dhid, item_dhid, user_dout, item_dout], axis=1)
    grads_copies = [
        send(
            grads.at[t], grads.at[t], grads_sems, k - 1, {"table": z_peers[k] * 2 + core}
        )
        for k in range(1, 4)
    ]
    pass_copies = [send(grads.at[t], grads.at[t], pass_sems, 0, {"table": sibling})]
    user_layer_t[...] = user_layer_ref[...].T
    item_layer_t[...] = item_layer_ref[...].T
    for k in range(1, 4):
        grads_copies[k - 1].wait_recv()
        slot = z_peers[k] * 2 + core
        pass_copies.append(
            send(grads.at[slot], grads.at[slot], pass_sems, k, {"table": sibling})
        )
    for copy in pass_copies:
        copy.wait_recv()
    for copy in slices_copies:
        copy.wait_recv()

    every = grads[...].reshape(128, 1280)
    kept = slices_in[...].reshape(128, 384)
    user_rows = dot_tn(kept[:, 0:128], every[:, 0:512]).astype(BF16)
    item_rows = dot_tn(kept[:, 128:256], every[:, 512:1024]).astype(BF16)
    head_rows = dot_tn(kept[:, 256:384], every[:, 1024:1280]).astype(BF16)
    for part in range(4):
        lanes = slice(part * 128, part * 128 + 128)
        tower_terms[part, 0:128, :] = user_rows[:, lanes]
        tower_terms[part, 128:256, :] = item_rows[:, lanes]
        tower_terms[part, 256:272, :] = head_rows[part * 16 : part * 16 + 16, 0:128]
        tower_terms[part, 272:288, :] = head_rows[64 + part * 16 : 80 + part * 16, 128:256]
    tower_copies = [
        send(
            tower_terms.at[dp_peers[k]], tower_in.at[k - 1], tower_sems, k - 1, {"dp": dp_peers[k]}
        )
        for k in range(1, 4)
    ]

    user_dpool = jnp.dot(
        every[:, 0:512], user_layer_t[...], preferred_element_type=F32
    ).astype(BF16)
    item_dpool = jnp.dot(
        every[:, 512:1024], item_layer_t[...], preferred_element_type=F32
    ).astype(BF16)
    columns = [user_dpool[:, f * 128 : f * 128 + 128] for f in range(8)] + [
        item_dpool[:, f * 128 : f * 128 + 128] for f in range(8)
    ]
    d_pooled = jnp.concatenate(columns, axis=0)
    for part in range(4):
        table_terms[part] = jnp.dot(
            weights[part * 256 : part * 256 + 256, :], d_pooled, preferred_element_type=F32
        ).astype(BF16)
    table_copies = [
        send(
            table_terms.at[dp_peers[k]], table_in.at[k - 1], table_sems, k - 1, {"dp": dp_peers[k]}
        )
        for k in range(1, 4)
    ]

    def gather_sum(terms, arrived, copies, result, sems):
        total = terms[d].astype(F32)
        for k in range(3):
            copies[k].wait_recv()
            total = total + arrived[k].astype(F32)
        result[d] = total.astype(BF16)
        return [
            send(result.at[d], result.at[d], sems, k - 1, {"dp": dp_peers[k]}) for k in range(1, 4)
        ]

    tower_all_copies = gather_sum(tower_terms, tower_in, tower_copies, tower_all, tower_all_sems)
    table_all_copies = gather_sum(table_terms, table_in, table_copies, table_all, table_all_sems)
    for copy in tower_all_copies:
        copy.wait_recv()
    for copy in table_all_copies:
        copy.wait_recv()
    for copy in (
        pair_copies
        + sums_copies
        + units_copies
        + slices_copies
        + grads_copies
        + pass_copies
        + tower_copies
        + table_copies
        + tower_all_copies
        + table_all_copies
    ):
        copy.wait_send()


def finish_kernel(
    losses_ref,
    tower_ref,
    table_ref,
    losses_out,
    table_out,
    user_layer_out,
    user_head_out,
    item_layer_out,
    item_head_out,
    table_wide,
    user_layer_wide,
    user_head_wide,
    item_layer_wide,
    item_head_wide,
    sems,
):
    copies = []

    def put(src, dst):
        copies.append(pltpu.make_async_copy(src, dst, sems.at[len(copies)]))
        copies[-1].start()

    put(losses_ref, losses_out)
    for part in range(4):
        table_wide[part * 256 : part * 256 + 256, :] = table_ref[part].astype(F32)
    put(table_wide, table_out)
    for part in range(4):
        lanes = slice(part * 128, part * 128 + 128)
        user_layer_wide[:, lanes] = tower_ref[part, 0:128, :].astype(F32)
    put(user_layer_wide, user_layer_out)
    for part in range(4):
        lanes = slice(part * 128, part * 128 + 128)
        item_layer_wide[:, lanes] = tower_ref[part, 128:256, :].astype(F32)
    put(item_layer_wide, item_layer_out)
    for part in range(4):
        rows = slice(part * 16, part * 16 + 16)
        user_head_wide[rows, :] = tower_ref[part, 256:272, :].astype(F32)
        item_head_wide[rows, :] = tower_ref[part, 272:288, :].astype(F32)
    put(user_head_wide, user_head_out)
    put(item_head_wide, item_head_out)
    for copy in copies:
        copy.wait()


def shards(ids, mults, table, user_layer, user_head, item_layer, item_head, counts):
    small = lax.axis_size("table") == 8 and lax.axis_size("dp") == 4
    if not small or ids.shape != (1, 128, 128) or table.shape != (1024, 128):
        return shards_general(
            ids, mults, table, user_layer, user_head, item_layer, item_head, counts
        )

    def dma(count):
        return pltpu.SemaphoreType.DMA((2, count))

    held = [
        pltpu.with_memory_space_constraint(x, pltpu.HBM)
        for x in (ids[0], mults[0], table, user_layer, user_head, item_layer, item_head, counts)
    ]
    vmem = pl.BlockSpec(memory_space=pltpu.VMEM)
    hbm = pl.BlockSpec(memory_space=pltpu.HBM)
    losses, tower_all, table_all = pl.pallas_call(
        step_kernel,
        out_shape=(
            jax.ShapeDtypeStruct((1, 16), F32),
            jax.ShapeDtypeStruct((4, 288, 128), BF16),
            jax.ShapeDtypeStruct((4, 256, 128), BF16),
        ),
        in_specs=[hbm] * 8,
        out_specs=(vmem,) * 3,
        scratch_shapes=[
            pltpu.VMEM((128, 128), jnp.int32),
            pltpu.VMEM((128, 128), jnp.int32),
            pltpu.VMEM((1024, 128), BF16),
            pltpu.VMEM((1024, 512), BF16),
            pltpu.VMEM((512, 128), BF16),
            pltpu.VMEM((1024, 512), BF16),
            pltpu.VMEM((512, 128), BF16),
            pltpu.VMEM((1, 16), jnp.int32),
            pltpu.VMEM((512, 1024), BF16),
            pltpu.VMEM((128, 512), BF16),
            pltpu.VMEM((512, 1024), BF16),
            pltpu.VMEM((128, 512), BF16),
            pltpu.VMEM((128, 128), jnp.int32),
            pltpu.VMEM((128, 128), jnp.int32),
            pltpu.VMEM((128, 1024), BF16),
            pltpu.VMEM((1024, 128), ROW_ID),
            pltpu.VMEM((1024, 2048), BF16),
            pltpu.VMEM((CHUNKS, 2, 4, 16, 512), BF16),
            pltpu.VMEM((CHUNKS, 4, 16, 512), BF16),
            pltpu.VMEM((CHUNKS, 4, 16, 512), BF16),
            pltpu.VMEM((CHUNKS, 3, 16, 512), BF16),
            pltpu.VMEM((8, 16, 384), BF16),
            pltpu.VMEM((8, 16, 384), BF16),
            pltpu.VMEM((4, 16, 384), BF16),
            pltpu.VMEM((8, 16, 1280), BF16),
            pltpu.VMEM((4, 288, 128), BF16),
            pltpu.VMEM((3, 288, 128), BF16),
            pltpu.VMEM((4, 256, 128), BF16),
            pltpu.VMEM((3, 256, 128), BF16),
            pltpu.SemaphoreType.DMA((8,)),
            dma(CHUNKS),
            dma(CHUNKS * 3),
            dma(7),
            dma(3),
            dma(3),
            dma(4),
            dma(3),
            dma(3),
            dma(3),
            dma(3),
        ],
        compiler_params=pltpu.CompilerParams(
            collective_id=0, has_side_effects=True, vmem_limit_bytes=40 * 1024 * 1024
        ),
        cost_estimate=pl.CostEstimate(
            flops=3_000_000_000, bytes_accessed=4_500_000, transcendentals=100_000
        ),
    )(*held)
    return pl.pallas_call(
        finish_kernel,
        out_shape=(
            jax.ShapeDtypeStruct((1, 16), F32),
            jax.ShapeDtypeStruct((1024, 128), F32),
            jax.ShapeDtypeStruct((128, 512), F32),
            jax.ShapeDtypeStruct((64, 128), F32),
            jax.ShapeDtypeStruct((128, 512), F32),
            jax.ShapeDtypeStruct((64, 128), F32),
        ),
        in_specs=[vmem] * 3,
        out_specs=(hbm,) * 6,
        scratch_shapes=[
            pltpu.VMEM((1024, 128), F32),
            pltpu.VMEM((128, 512), F32),
            pltpu.VMEM((64, 128), F32),
            pltpu.VMEM((128, 512), F32),
            pltpu.VMEM((64, 128), F32),
            pltpu.SemaphoreType.DMA((6,)),
        ],
        compiler_params=pltpu.CompilerParams(vmem_limit_bytes=16 * 1024 * 1024),
    )(losses, tower_all, table_all)


def solution(mesh):
    in_specs = (
        P("table", "dp", None),
        P("table", "dp", None),
        P("table", None),
        P(),
        P(),
        P(),
        P(),
        P("dp", "table"),
    )
    out_specs = (
        P("dp", "table"),
        P("table", None),
        P("table", None),
        P("table", None),
        P("table", None),
        P("table", None),
    )
    return jax.shard_map(shards, mesh=mesh, in_specs=in_specs, out_specs=out_specs, check_vma=False)
```

```python
import functools

import jax
import jax.numpy as jnp
from jax import lax
from jax.experimental import pallas as pl
from jax.experimental.pallas import tpu as pltpu
from jax.sharding import PartitionSpec as P

LOOKUPS = 8


INVERSE_TEMP = 20.0
EPSILON = 1e-06


def silu_slope(pre):
    gate = jax.nn.sigmoid(pre)
    return gate * (1.0 + pre * (1.0 - gate))


def run_tower(pooled_in, layer, head):
    pre = jnp.dot(pooled_in, layer, preferred_element_type=jnp.float32)
    hidden = jax.nn.silu(pre).astype(jnp.bfloat16)
    output = jnp.dot(hidden, head, preferred_element_type=jnp.float32)
    scale = lax.rsqrt(jnp.sum(output * output, axis=-1, keepdims=True) + EPSILON)
    return (pre, hidden, output * scale, scale)


def tower_back(d_unit, unit, scale, pre, hidden, pooled_in, head):
    along = jnp.sum(unit * d_unit, axis=-1, keepdims=True)
    d_output = ((d_unit - unit * along) * scale).astype(jnp.bfloat16)
    back = lax.dot_general(
        d_output, head, (((1,), (1,)), ((), ())), preferred_element_type=jnp.float32
    )
    d_hidden = (back * silu_slope(pre)).astype(jnp.bfloat16)
    layer_term = lax.dot_general(
        pooled_in, d_hidden, (((0,), (0,)), ((), ())), preferred_element_type=jnp.float32
    )
    head_term = lax.dot_general(
        hidden, d_output, (((0,), (0,)), ((), ())), preferred_element_type=jnp.float32
    )
    return (d_output, d_hidden, layer_term, head_term)


def input_grads(d_hidden, layer):
    return lax.dot_general(
        d_hidden, layer, (((1,), (1,)), ((), ())), preferred_element_type=jnp.float32
    ).astype(jnp.bfloat16)


def shards_general(ids, mults, table, user_layer, user_head, item_layer, item_head, counts):
    table_count = lax.axis_size("table")
    rows_dev, emb_width = table.shape
    group_rows = ids.shape[1]
    feature_count = ids.shape[2] // LOOKUPS
    own_rows = group_rows // table_count
    user_width = user_layer.shape[0]
    id_blocks = ids[0].reshape(group_rows, feature_count, LOOKUPS).transpose(1, 0, 2)
    mult_blocks = mults[0].reshape(group_rows, feature_count, LOOKUPS).transpose(1, 0, 2)
    table_rows = lax.broadcasted_iota(jnp.int32, (1, rows_dev), 1)

    def lookup_weights(id_block, mult_block):
        running = jnp.zeros((group_rows, rows_dev), jnp.float32)
        for lookup in range(LOOKUPS):
            hit = id_block[:, lookup : lookup + 1] == table_rows
            running = running + jnp.where(
                hit, mult_block[:, lookup : lookup + 1].astype(jnp.float32), 0.0
            )
        return running.astype(jnp.bfloat16)

    def pool_feature(lookup_pair):
        weights = lookup_weights(lookup_pair[0], lookup_pair[1])
        return jnp.dot(weights, table, preferred_element_type=jnp.float32).astype(jnp.bfloat16)

    partial_value = lax.map(pool_feature, (id_blocks, mult_blocks))
    received = lax.all_to_all(partial_value, "table", split_axis=1, concat_axis=1, tiled=True)
    pooled = jnp.sum(
        received.astype(jnp.float32).reshape(feature_count, table_count, own_rows, emb_width),
        axis=1,
    ).astype(jnp.bfloat16)
    pooled = pooled.transpose(1, 0, 2).reshape(own_rows, feature_count * emb_width)
    user_in = pooled[:, :user_width]
    item_in = pooled[:, user_width:]
    user_pre, user_hidden, user_unit, user_scale = run_tower(user_in, user_layer, user_head)
    item_pre, item_hidden, item_unit, item_scale = run_tower(item_in, item_layer, item_head)
    user_vector = user_unit.astype(jnp.bfloat16)
    item_vector = item_unit.astype(jnp.bfloat16)
    item_rows, item_counts = (
        lax.all_gather(item_vector, "dp", axis=0, tiled=True),
        lax.all_gather(counts[0].astype(jnp.bfloat16), "dp", axis=0, tiled=True),
    )
    log_freq = jnp.log(item_counts.astype(jnp.float32))
    scores = (
        INVERSE_TEMP
        * lax.dot_general(
            user_vector, item_rows, (((1,), (1,)), ((), ())), preferred_element_type=jnp.float32
        )
        - log_freq[None, :]
    )
    lse = jnp.log(jnp.sum(jnp.exp(scores), axis=-1))
    own_index = lax.axis_index("dp") * own_rows + lax.broadcasted_iota(jnp.int32, (own_rows,), 0)
    columns = lax.broadcasted_iota(jnp.int32, scores.shape, 1)
    is_positive = columns == own_index[:, None]
    positive = jnp.sum(jnp.where(is_positive, scores, 0.0), axis=-1)
    losses = (lse - positive)[None, :]
    dscore = (jnp.exp(scores - lse[:, None]) - is_positive.astype(jnp.float32)).astype(jnp.bfloat16)
    d_user = INVERSE_TEMP * jnp.dot(dscore, item_rows, preferred_element_type=jnp.float32)
    item_terms = INVERSE_TEMP * lax.dot_general(
        dscore, user_vector, (((0,), (0,)), ((), ())), preferred_element_type=jnp.float32
    )
    d_item = lax.psum_scatter(
        item_terms.astype(jnp.bfloat16), "dp", scatter_dimension=0, tiled=True
    ).astype(jnp.float32)
    user_dout, user_dhid, user_layer_term, user_head_term = tower_back(
        d_user, user_unit, user_scale, user_pre, user_hidden, user_in, user_head
    )
    item_dout, item_dhid, item_layer_term, item_head_term = tower_back(
        d_item, item_unit, item_scale, item_pre, item_hidden, item_in, item_head
    )
    own_grads = jnp.concatenate(
        [input_grads(user_dhid, user_layer), input_grads(item_dhid, item_layer)], axis=1
    )
    group_grads = lax.all_gather(own_grads, "table", axis=0, tiled=True)

    def add_feature(feature, running):
        weights = lookup_weights(id_blocks[feature], mult_blocks[feature])
        column = lax.dynamic_slice_in_dim(group_grads, feature * emb_width, emb_width, 1)
        return running + lax.dot_general(
            weights, column, (((0,), (0,)), ((), ())), preferred_element_type=jnp.float32
        )

    table_part = lax.fori_loop(
        0, feature_count, add_feature, jnp.zeros((rows_dev, emb_width), jnp.float32)
    )
    layer_rows = (
        lax.psum_scatter(
            user_layer_term.astype(jnp.bfloat16), "table", scatter_dimension=0, tiled=True
        ).astype(jnp.float32),
        lax.psum_scatter(
            user_head_term.astype(jnp.bfloat16), "table", scatter_dimension=0, tiled=True
        ).astype(jnp.float32),
        lax.psum_scatter(
            item_layer_term.astype(jnp.bfloat16), "table", scatter_dimension=0, tiled=True
        ).astype(jnp.float32),
        lax.psum_scatter(
            item_head_term.astype(jnp.bfloat16), "table", scatter_dimension=0, tiled=True
        ).astype(jnp.float32),
    )
    totals = (
        lax.psum(table_part.astype(jnp.bfloat16), "dp").astype(jnp.float32),
        lax.psum(layer_rows[0].astype(jnp.bfloat16), "dp").astype(jnp.float32),
        lax.psum(layer_rows[1].astype(jnp.bfloat16), "dp").astype(jnp.float32),
        lax.psum(layer_rows[2].astype(jnp.bfloat16), "dp").astype(jnp.float32),
        lax.psum(layer_rows[3].astype(jnp.bfloat16), "dp").astype(jnp.float32),
    )
    return (losses, totals[0], totals[1], totals[2], totals[3], totals[4])


BF16 = jnp.bfloat16
F32 = jnp.float32
ROW_ID = jnp.int16
CHUNKS = 4
MESH = pl.DeviceIdType.MESH


def flip(value, mask, bits):
    out = 0
    for bit in range(bits):
        one = lax.rem(lax.div(value, 1 << bit), 2)
        if (mask >> bit) & 1:
            one = 1 - one
        out = out + one * (1 << bit)
    return out


def dot_nt(left, right):
    return lax.dot_general(left, right, (((1,), (1,)), ((), ())), preferred_element_type=F32)


def dot_tn(left, right):
    return lax.dot_general(left, right, (((0,), (0,)), ((), ())), preferred_element_type=F32)


def step_kernel(
    ids_hbm,
    mults_hbm,
    table_hbm,
    user_layer_hbm,
    user_head_hbm,
    item_layer_hbm,
    item_head_hbm,
    counts_hbm,
    losses_ref,
    tower_all,
    table_all,
    ids_ref,
    mults_ref,
    table_ref,
    user_layer_ref,
    user_head_ref,
    item_layer_ref,
    item_head_ref,
    counts_ref,
    user_layer_t,
    user_head_t,
    item_layer_t,
    item_head_t,
    ids_t,
    mults_t,
    table_t,
    row_ids,
    weights,
    parts,
    pair_in,
    sums,
    sums_in,
    slices,
    slices_in,
    units,
    grads,
    tower_terms,
    tower_in,
    tower_mid,
    tower_second,
    table_terms,
    table_in,
    table_mid,
    table_second,
    load_sems,
    pair_sems,
    sums_sems,
    slices_sems,
    units_sems,
    grads_sems,
    pass_sems,
    tower_sems,
    tower_all_sems,
    table_sems,
    table_all_sems,
):
    pairs = (
        (ids_hbm, ids_ref),
        (mults_hbm, mults_ref),
        (table_hbm, table_ref),
        (user_layer_hbm, user_layer_ref),
        (item_layer_hbm, item_layer_ref),
        (user_head_hbm, user_head_ref),
        (item_head_hbm, item_head_ref),
        (counts_hbm, counts_ref),
    )
    loads = [pltpu.make_async_copy(a, b, load_sems.at[i]) for i, (a, b) in enumerate(pairs)]
    for load in loads:
        load.start()
    t = lax.axis_index("table")
    d = lax.axis_index("dp")
    z = lax.div(t, 2)
    core = lax.rem(t, 2)
    sibling = z * 2 + (1 - core)
    z_peers = [flip(z, k, 2) for k in range(4)]
    dp_peers = [flip(d, k, 2) for k in range(4)]

    barrier = pltpu.get_barrier_semaphore()
    for k in range(1, 8):
        pl.semaphore_signal(barrier, inc=1, device_id={"table": flip(t, k, 3)}, device_id_type=MESH)
    for k in range(1, 4):
        pl.semaphore_signal(barrier, inc=1, device_id={"dp": dp_peers[k]}, device_id_type=MESH)

    def send(src, dst, sems, index, target):
        copy = pltpu.make_async_remote_copy(
            src_ref=src,
            dst_ref=dst,
            send_sem=sems.at[0, index],
            recv_sem=sems.at[1, index],
            device_id=target,
            device_id_type=MESH,
        )
        copy.start()
        return copy

    row_ids[...] = lax.broadcasted_iota(jnp.int32, row_ids.shape, 0).astype(row_ids.dtype)
    for load in loads[:3]:
        load.wait()
    ids_t[...] = ids_ref[...].T
    mults_t[...] = mults_ref[...].T
    table_t[...] = table_ref[...].T
    block = 128

    def pool_pair(chunk, pair):
        for half in range(2):
            feature = chunk * 4 + pair * 2 + half
            slots = pl.ds(pl.multiple_of(feature * 8, 8), 8)
            id_rows = ids_t[slots, :]
            mult_rows = mults_t[slots, :].astype(F32)
            spread = [
                (
                    jnp.broadcast_to(id_rows[l : l + 1, :], (16, 128)).astype(row_ids.dtype),
                    jnp.broadcast_to(mult_rows[l : l + 1, :], (16, 128)).astype(BF16),
                )
                for l in range(LOOKUPS)
            ]
            lanes = pl.ds(pl.multiple_of(feature * 128, 128), 128)
            for start in range(0, 1024, block):
                here = row_ids[start : start + block, :].reshape(block // 16, 16, 128)
                total = None
                for id_row, mult_row in spread:
                    term = jnp.where(here == id_row[None], mult_row[None], jnp.zeros((), BF16))
                    total = term if total is None else total + term
                weights[start : start + block, lanes] = total.reshape(block, 128)
        lanes = pl.ds(pl.multiple_of((chunk * 4 + pair * 2) * 128, 256), 256)
        pooled_t = jnp.dot(table_t[...], weights[:, lanes], preferred_element_type=F32)
        for half in range(2):
            pooled = pooled_t[:, half * 128 : half * 128 + 128].T.astype(BF16)
            place = pl.ds(pl.multiple_of((pair * 2 + half) * 128, 128), 128)
            for owner in range(8):
                parts[chunk, owner % 2, owner // 2, :, place] = pooled[owner * 16 : owner * 16 + 16]

    pair_copies, sums_copies = [], []

    def pass_on(chunk):
        pair_copies[chunk].wait_recv()
        total = parts[chunk, core].astype(F32) + pair_in[chunk].astype(F32)
        sums[chunk] = total.astype(BF16)
        for k in range(1, 4):
            sums_copies.append(
                send(
                    sums.at[chunk, z_peers[k]],
                    sums_in.at[chunk, k - 1],
                    sums_sems,
                    chunk * 3 + k - 1,
                    {"table": z_peers[k] * 2 + core},
                )
            )

    for chunk in range(CHUNKS):

        def pool_step(pair, carry):
            pool_pair(chunk, pair)
            return carry

        lax.fori_loop(0, 2, pool_step, 0)
        if chunk == 0:
            pl.semaphore_wait(barrier, 10)
        pair_copies.append(
            send(
                parts.at[chunk, 1 - core],
                pair_in.at[chunk],
                pair_sems,
                chunk,
                {"table": sibling},
            )
        )
        if chunk > 0:
            pass_on(chunk - 1)
    for load in loads[3:]:
        load.wait()
    pass_on(CHUNKS - 1)
    user_head_t[...] = user_head_ref[...].T
    item_head_t[...] = item_head_ref[...].T
    pooled = []
    for chunk in range(CHUNKS):
        total = sums[chunk, z].astype(F32)
        for k in range(3):
            sums_copies[chunk * 3 + k].wait_recv()
            total = total + sums_in[chunk, k].astype(F32)
        pooled.append(total.astype(BF16))
    user_in = jnp.concatenate(pooled[:2], axis=1)
    item_in = jnp.concatenate(pooled[2:], axis=1)

    user_pre, user_hidden, user_unit, user_scale = run_tower(
        user_in, user_layer_ref[...], user_head_ref[...]
    )
    item_pre, item_hidden, item_unit, item_scale = run_tower(
        item_in, item_layer_ref[...], item_head_ref[...]
    )
    eye16 = lax.broadcasted_iota(jnp.int32, (16, 16), 0) == lax.broadcasted_iota(
        jnp.int32, (16, 16), 1
    )
    count_column = jnp.sum(
        jnp.where(eye16, jnp.broadcast_to(counts_ref[...].astype(F32), (16, 16)), 0.0),
        axis=1,
        keepdims=True,
    )
    units[0, :, 0:128] = user_unit.astype(BF16)
    units[0, :, 128:256] = item_unit.astype(BF16)
    units[0, :, 256:384] = jnp.broadcast_to(count_column, (16, 128)).astype(BF16)
    units_copies = [
        send(units.at[0], units.at[k], units_sems, k - 1, {"dp": dp_peers[k]}) for k in range(1, 4)
    ]
    for owner in range(8):
        slices[owner, :, 0:128] = user_in[:, owner * 128 : owner * 128 + 128]
        slices[owner, :, 128:256] = item_in[:, owner * 128 : owner * 128 + 128]
        slices[owner, :, 256:384] = jnp.concatenate(
            [
                user_hidden[:, owner * 64 : owner * 64 + 64],
                item_hidden[:, owner * 64 : owner * 64 + 64],
            ],
            axis=1,
        )
    slices_copies = []
    for k in range(1, 8):
        peer = flip(t, k, 3)
        slices_copies.append(
            send(slices.at[peer], slices_in.at[t], slices_sems, k - 1, {"table": peer})
        )
    slices_in[t] = slices[t]
    for copy in units_copies:
        copy.wait_recv()

    every = units[...]
    users = every[:, :, 0:128].reshape(64, 128)
    items = every[:, :, 128:256].reshape(64, 128)
    log_freq = jnp.log(every[:, :, 256:384].reshape(64, 128).astype(F32))[:, 0:1]
    scores = INVERSE_TEMP * dot_nt(items, users) - log_freq
    lse = jnp.log(jnp.sum(jnp.exp(scores), axis=0, keepdims=True))
    same = lax.broadcasted_iota(jnp.int32, (64, 64), 0) == lax.broadcasted_iota(
        jnp.int32, (64, 64), 1
    )
    positive = jnp.sum(jnp.where(same, scores, 0.0), axis=0, keepdims=True)
    losses_ref[...] = (lse - positive)[:, 0:16]
    dscore = (jnp.exp(scores - lse) - jnp.where(same, 1.0, 0.0)).astype(BF16)
    d_user = INVERSE_TEMP * dot_tn(dscore, items)[0:16]
    d_item = INVERSE_TEMP * jnp.dot(dscore[0:16], users, preferred_element_type=F32)

    def back(d_unit, unit, scale, pre, head_t):
        along = jnp.sum(unit * d_unit, axis=-1, keepdims=True)
        d_output = ((d_unit - unit * along) * scale).astype(BF16)
        d_hidden = (
            jnp.dot(d_output, head_t[...], preferred_element_type=F32) * silu_slope(pre)
        ).astype(BF16)
        return d_output, d_hidden

    user_dout, user_dhid = back(d_user, user_unit, user_scale, user_pre, user_head_t)
    item_dout, item_dhid = back(d_item, item_unit, item_scale, item_pre, item_head_t)
    grads[t] = jnp.concatenate([user_dhid, item_dhid, user_dout, item_dout], axis=1)
    grads_copies = [
        send(
            grads.at[t], grads.at[t], grads_sems, k - 1, {"table": z_peers[k] * 2 + core}
        )
        for k in range(1, 4)
    ]
    pass_copies = [send(grads.at[t], grads.at[t], pass_sems, 0, {"table": sibling})]
    user_layer_t[...] = user_layer_ref[...].T
    item_layer_t[...] = item_layer_ref[...].T
    for k in range(1, 4):
        grads_copies[k - 1].wait_recv()
        slot = z_peers[k] * 2 + core
        pass_copies.append(
            send(grads.at[slot], grads.at[slot], pass_sems, k, {"table": sibling})
        )
    for copy in pass_copies:
        copy.wait_recv()
    for copy in slices_copies:
        copy.wait_recv()

    every = grads[...].reshape(128, 1280)
    kept = slices_in[...].reshape(128, 384)
    user_rows = dot_tn(kept[:, 0:128], every[:, 0:512]).astype(BF16)
    item_rows = dot_tn(kept[:, 128:256], every[:, 512:1024]).astype(BF16)
    head_rows = dot_tn(kept[:, 256:384], every[:, 1024:1280]).astype(BF16)
    for part in range(4):
        lanes = slice(part * 128, part * 128 + 128)
        tower_terms[part, 0, 0:128, :] = user_rows[:, lanes]
        tower_terms[part, 0, 128:144, :] = head_rows[part * 16 : part * 16 + 16, 0:128]
        tower_terms[part, 1, 0:128, :] = item_rows[:, lanes]
        tower_terms[part, 1, 128:144, :] = head_rows[64 + part * 16 : 80 + part * 16, 128:256]

    by_x, by_y, across = dp_peers[1], dp_peers[2], dp_peers[3]

    def scatter_start(terms, first, sems):
        return [
            send(terms.at[across, 0], first.at[0, 1], sems, 0, {"dp": by_x}),
            send(terms.at[across, 1], first.at[1, 1], sems, 1, {"dp": by_y}),
            send(terms.at[by_x, 0], first.at[0, 0], sems, 2, {"dp": by_x}),
            send(terms.at[by_y, 1], first.at[1, 0], sems, 3, {"dp": by_y}),
        ]

    def scatter_pass(terms, first, middle, second, copies, sems):
        for half, target in ((0, by_y), (1, by_x)):
            copies[half].wait_recv()
            total = terms[target, half].astype(F32) + first[half, 1].astype(F32)
            middle[half] = total.astype(BF16)
            copies.append(
                send(middle.at[half], second.at[half], sems, 4 + half, {"dp": target})
            )

    def gather_start(terms, first, second, copies, result, sems):
        for half in range(2):
            copies[2 + half].wait_recv()
            copies[4 + half].wait_recv()
            total = terms[d, half].astype(F32) + first[half, 0].astype(F32)
            result[d, half] = (total + second[half].astype(F32)).astype(BF16)
        own = [result.at[d, 0], result.at[d, 1]]
        return [
            send(own[0], own[0], sems, 0, {"dp": by_y}),
            send(own[1], own[1], sems, 1, {"dp": by_x}),
            send(own[0], own[0], sems, 2, {"dp": by_x}),
            send(own[1], own[1], sems, 3, {"dp": by_y}),
        ]

    def gather_pass(copies, result, sems):
        for half, source, target in ((0, by_y, by_x), (1, by_x, by_y)):
            copies[half].wait_recv()
            held = result.at[source, half]
            copies.append(send(held, held, sems, 4 + half, {"dp": target}))

    tower_copies = scatter_start(tower_terms, tower_in, tower_sems)

    user_dpool = jnp.dot(
        every[:, 0:512], user_layer_t[...], preferred_element_type=F32
    ).astype(BF16)
    item_dpool = jnp.dot(
        every[:, 512:1024], item_layer_t[...], preferred_element_type=F32
    ).astype(BF16)
    columns = [user_dpool[:, f * 128 : f * 128 + 128] for f in range(8)] + [
        item_dpool[:, f * 128 : f * 128 + 128] for f in range(8)
    ]
    d_pooled = jnp.concatenate(columns, axis=0)
    for part in range(4):
        table_terms[part] = (
            jnp.dot(
                weights[part * 256 : part * 256 + 256, :], d_pooled, preferred_element_type=F32
            )
            .astype(BF16)
            .reshape(2, 128, 128)
        )
    table_copies = scatter_start(table_terms, table_in, table_sems)
    scatter_pass(tower_terms, tower_in, tower_mid, tower_second, tower_copies, tower_sems)
    scatter_pass(table_terms, table_in, table_mid, table_second, table_copies, table_sems)
    tower_all_copies = gather_start(
        tower_terms, tower_in, tower_second, tower_copies, tower_all, tower_all_sems
    )
    table_all_copies = gather_start(
        table_terms, table_in, table_second, table_copies, table_all, table_all_sems
    )
    gather_pass(tower_all_copies, tower_all, tower_all_sems)
    gather_pass(table_all_copies, table_all, table_all_sems)
    for copy in tower_all_copies[2:] + table_all_copies[2:]:
        copy.wait_recv()
    for copy in (
        pair_copies
        + sums_copies
        + units_copies
        + slices_copies
        + grads_copies
        + pass_copies
        + tower_copies
        + table_copies
        + tower_all_copies
        + table_all_copies
    ):
        copy.wait_send()


def finish_kernel(
    losses_ref,
    tower_ref,
    table_ref,
    losses_out,
    table_out,
    user_layer_out,
    user_head_out,
    item_layer_out,
    item_head_out,
    table_wide,
    user_layer_wide,
    user_head_wide,
    item_layer_wide,
    item_head_wide,
    sems,
):
    copies = []

    def put(src, dst):
        copies.append(pltpu.make_async_copy(src, dst, sems.at[len(copies)]))
        copies[-1].start()

    put(losses_ref, losses_out)
    for part in range(4):
        table_wide[part * 256 : part * 256 + 256, :] = table_ref[part].reshape(256, 128).astype(F32)
    put(table_wide, table_out)
    for part in range(4):
        lanes = slice(part * 128, part * 128 + 128)
        user_layer_wide[:, lanes] = tower_ref[part, 0, 0:128, :].astype(F32)
    put(user_layer_wide, user_layer_out)
    for part in range(4):
        lanes = slice(part * 128, part * 128 + 128)
        item_layer_wide[:, lanes] = tower_ref[part, 1, 0:128, :].astype(F32)
    put(item_layer_wide, item_layer_out)
    for part in range(4):
        rows = slice(part * 16, part * 16 + 16)
        user_head_wide[rows, :] = tower_ref[part, 0, 128:144, :].astype(F32)
        item_head_wide[rows, :] = tower_ref[part, 1, 128:144, :].astype(F32)
    put(user_head_wide, user_head_out)
    put(item_head_wide, item_head_out)
    for copy in copies:
        copy.wait()


def shards(ids, mults, table, user_layer, user_head, item_layer, item_head, counts):
    small = lax.axis_size("table") == 8 and lax.axis_size("dp") == 4
    if not small or ids.shape != (1, 128, 128) or table.shape != (1024, 128):
        return shards_general(
            ids, mults, table, user_layer, user_head, item_layer, item_head, counts
        )

    def dma(count):
        return pltpu.SemaphoreType.DMA((2, count))

    held = [
        pltpu.with_memory_space_constraint(x, pltpu.HBM)
        for x in (ids[0], mults[0], table, user_layer, user_head, item_layer, item_head, counts)
    ]
    vmem = pl.BlockSpec(memory_space=pltpu.VMEM)
    hbm = pl.BlockSpec(memory_space=pltpu.HBM)
    losses, tower_all, table_all = pl.pallas_call(
        step_kernel,
        out_shape=(
            jax.ShapeDtypeStruct((1, 16), F32),
            jax.ShapeDtypeStruct((4, 2, 144, 128), BF16),
            jax.ShapeDtypeStruct((4, 2, 128, 128), BF16),
        ),
        in_specs=[hbm] * 8,
        out_specs=(vmem,) * 3,
        scratch_shapes=[
            pltpu.VMEM((128, 128), jnp.int32),
            pltpu.VMEM((128, 128), jnp.int32),
            pltpu.VMEM((1024, 128), BF16),
            pltpu.VMEM((1024, 512), BF16),
            pltpu.VMEM((512, 128), BF16),
            pltpu.VMEM((1024, 512), BF16),
            pltpu.VMEM((512, 128), BF16),
            pltpu.VMEM((1, 16), jnp.int32),
            pltpu.VMEM((512, 1024), BF16),
            pltpu.VMEM((128, 512), BF16),
            pltpu.VMEM((512, 1024), BF16),
            pltpu.VMEM((128, 512), BF16),
            pltpu.VMEM((128, 128), jnp.int32),
            pltpu.VMEM((128, 128), jnp.int32),
            pltpu.VMEM((128, 1024), BF16),
            pltpu.VMEM((1024, 128), ROW_ID),
            pltpu.VMEM((1024, 2048), BF16),
            pltpu.VMEM((CHUNKS, 2, 4, 16, 512), BF16),
            pltpu.VMEM((CHUNKS, 4, 16, 512), BF16),
            pltpu.VMEM((CHUNKS, 4, 16, 512), BF16),
            pltpu.VMEM((CHUNKS, 3, 16, 512), BF16),
            pltpu.VMEM((8, 16, 384), BF16),
            pltpu.VMEM((8, 16, 384), BF16),
            pltpu.VMEM((4, 16, 384), BF16),
            pltpu.VMEM((8, 16, 1280), BF16),
            pltpu.VMEM((4, 2, 144, 128), BF16),
            pltpu.VMEM((2, 2, 144, 128), BF16),
            pltpu.VMEM((2, 144, 128), BF16),
            pltpu.VMEM((2, 144, 128), BF16),
            pltpu.VMEM((4, 2, 128, 128), BF16),
            pltpu.VMEM((2, 2, 128, 128), BF16),
            pltpu.VMEM((2, 128, 128), BF16),
            pltpu.VMEM((2, 128, 128), BF16),
            pltpu.SemaphoreType.DMA((8,)),
            dma(CHUNKS),
            dma(CHUNKS * 3),
            dma(7),
            dma(3),
            dma(3),
            dma(4),
            dma(6),
            dma(6),
            dma(6),
            dma(6),
        ],
        compiler_params=pltpu.CompilerParams(
            collective_id=0, has_side_effects=True, vmem_limit_bytes=40 * 1024 * 1024
        ),
        cost_estimate=pl.CostEstimate(
            flops=3_000_000_000, bytes_accessed=4_500_000, transcendentals=100_000
        ),
    )(*held)
    return pl.pallas_call(
        finish_kernel,
        out_shape=(
            jax.ShapeDtypeStruct((1, 16), F32),
            jax.ShapeDtypeStruct((1024, 128), F32),
            jax.ShapeDtypeStruct((128, 512), F32),
            jax.ShapeDtypeStruct((64, 128), F32),
            jax.ShapeDtypeStruct((128, 512), F32),
            jax.ShapeDtypeStruct((64, 128), F32),
        ),
        in_specs=[vmem] * 3,
        out_specs=(hbm,) * 6,
        scratch_shapes=[
            pltpu.VMEM((1024, 128), F32),
            pltpu.VMEM((128, 512), F32),
            pltpu.VMEM((64, 128), F32),
            pltpu.VMEM((128, 512), F32),
            pltpu.VMEM((64, 128), F32),
            pltpu.SemaphoreType.DMA((6,)),
        ],
        compiler_params=pltpu.CompilerParams(vmem_limit_bytes=16 * 1024 * 1024),
    )(losses, tower_all, table_all)


def solution(mesh):
    in_specs = (
        P("table", "dp", None),
        P("table", "dp", None),
        P("table", None),
        P(),
        P(),
        P(),
        P(),
        P("dp", "table"),
    )
    out_specs = (
        P("dp", "table"),
        P("table", None),
        P("table", None),
        P("table", None),
        P("table", None),
        P("table", None),
    )
    return jax.shard_map(shards, mesh=mesh, in_specs=in_specs, out_specs=out_specs, check_vma=False)
```

```python
import functools

import jax
import jax.numpy as jnp
from jax import lax
from jax.experimental import pallas as pl
from jax.experimental.pallas import tpu as pltpu
from jax.sharding import PartitionSpec as P

LOOKUPS = 8


INVERSE_TEMP = 20.0
EPSILON = 1e-06


def silu_slope(pre):
    gate = jax.nn.sigmoid(pre)
    return gate * (1.0 + pre * (1.0 - gate))


def run_tower(pooled_in, layer, head):
    pre = jnp.dot(pooled_in, layer, preferred_element_type=jnp.float32)
    hidden = jax.nn.silu(pre).astype(jnp.bfloat16)
    output = jnp.dot(hidden, head, preferred_element_type=jnp.float32)
    scale = lax.rsqrt(jnp.sum(output * output, axis=-1, keepdims=True) + EPSILON)
    return (pre, hidden, output * scale, scale)


def tower_back(d_unit, unit, scale, pre, hidden, pooled_in, head):
    along = jnp.sum(unit * d_unit, axis=-1, keepdims=True)
    d_output = ((d_unit - unit * along) * scale).astype(jnp.bfloat16)
    back = lax.dot_general(
        d_output, head, (((1,), (1,)), ((), ())), preferred_element_type=jnp.float32
    )
    d_hidden = (back * silu_slope(pre)).astype(jnp.bfloat16)
    layer_term = lax.dot_general(
        pooled_in, d_hidden, (((0,), (0,)), ((), ())), preferred_element_type=jnp.float32
    )
    head_term = lax.dot_general(
        hidden, d_output, (((0,), (0,)), ((), ())), preferred_element_type=jnp.float32
    )
    return (d_output, d_hidden, layer_term, head_term)


def input_grads(d_hidden, layer):
    return lax.dot_general(
        d_hidden, layer, (((1,), (1,)), ((), ())), preferred_element_type=jnp.float32
    ).astype(jnp.bfloat16)


def shards_general(ids, mults, table, user_layer, user_head, item_layer, item_head, counts):
    table_count = lax.axis_size("table")
    rows_dev, emb_width = table.shape
    group_rows = ids.shape[1]
    feature_count = ids.shape[2] // LOOKUPS
    own_rows = group_rows // table_count
    user_width = user_layer.shape[0]
    id_blocks = ids[0].reshape(group_rows, feature_count, LOOKUPS).transpose(1, 0, 2)
    mult_blocks = mults[0].reshape(group_rows, feature_count, LOOKUPS).transpose(1, 0, 2)
    table_rows = lax.broadcasted_iota(jnp.int32, (1, rows_dev), 1)

    def lookup_weights(id_block, mult_block):
        running = jnp.zeros((group_rows, rows_dev), jnp.float32)
        for lookup in range(LOOKUPS):
            hit = id_block[:, lookup : lookup + 1] == table_rows
            running = running + jnp.where(
                hit, mult_block[:, lookup : lookup + 1].astype(jnp.float32), 0.0
            )
        return running.astype(jnp.bfloat16)

    def pool_feature(lookup_pair):
        weights = lookup_weights(lookup_pair[0], lookup_pair[1])
        return jnp.dot(weights, table, preferred_element_type=jnp.float32).astype(jnp.bfloat16)

    partial_value = lax.map(pool_feature, (id_blocks, mult_blocks))
    received = lax.all_to_all(partial_value, "table", split_axis=1, concat_axis=1, tiled=True)
    pooled = jnp.sum(
        received.astype(jnp.float32).reshape(feature_count, table_count, own_rows, emb_width),
        axis=1,
    ).astype(jnp.bfloat16)
    pooled = pooled.transpose(1, 0, 2).reshape(own_rows, feature_count * emb_width)
    user_in = pooled[:, :user_width]
    item_in = pooled[:, user_width:]
    user_pre, user_hidden, user_unit, user_scale = run_tower(user_in, user_layer, user_head)
    item_pre, item_hidden, item_unit, item_scale = run_tower(item_in, item_layer, item_head)
    user_vector = user_unit.astype(jnp.bfloat16)
    item_vector = item_unit.astype(jnp.bfloat16)
    item_rows, item_counts = (
        lax.all_gather(item_vector, "dp", axis=0, tiled=True),
        lax.all_gather(counts[0].astype(jnp.bfloat16), "dp", axis=0, tiled=True),
    )
    log_freq = jnp.log(item_counts.astype(jnp.float32))
    scores = (
        INVERSE_TEMP
        * lax.dot_general(
            user_vector, item_rows, (((1,), (1,)), ((), ())), preferred_element_type=jnp.float32
        )
        - log_freq[None, :]
    )
    lse = jnp.log(jnp.sum(jnp.exp(scores), axis=-1))
    own_index = lax.axis_index("dp") * own_rows + lax.broadcasted_iota(jnp.int32, (own_rows,), 0)
    columns = lax.broadcasted_iota(jnp.int32, scores.shape, 1)
    is_positive = columns == own_index[:, None]
    positive = jnp.sum(jnp.where(is_positive, scores, 0.0), axis=-1)
    losses = (lse - positive)[None, :]
    dscore = (jnp.exp(scores - lse[:, None]) - is_positive.astype(jnp.float32)).astype(jnp.bfloat16)
    d_user = INVERSE_TEMP * jnp.dot(dscore, item_rows, preferred_element_type=jnp.float32)
    item_terms = INVERSE_TEMP * lax.dot_general(
        dscore, user_vector, (((0,), (0,)), ((), ())), preferred_element_type=jnp.float32
    )
    d_item = lax.psum_scatter(
        item_terms.astype(jnp.bfloat16), "dp", scatter_dimension=0, tiled=True
    ).astype(jnp.float32)
    user_dout, user_dhid, user_layer_term, user_head_term = tower_back(
        d_user, user_unit, user_scale, user_pre, user_hidden, user_in, user_head
    )
    item_dout, item_dhid, item_layer_term, item_head_term = tower_back(
        d_item, item_unit, item_scale, item_pre, item_hidden, item_in, item_head
    )
    own_grads = jnp.concatenate(
        [input_grads(user_dhid, user_layer), input_grads(item_dhid, item_layer)], axis=1
    )
    group_grads = lax.all_gather(own_grads, "table", axis=0, tiled=True)

    def add_feature(feature, running):
        weights = lookup_weights(id_blocks[feature], mult_blocks[feature])
        column = lax.dynamic_slice_in_dim(group_grads, feature * emb_width, emb_width, 1)
        return running + lax.dot_general(
            weights, column, (((0,), (0,)), ((), ())), preferred_element_type=jnp.float32
        )

    table_part = lax.fori_loop(
        0, feature_count, add_feature, jnp.zeros((rows_dev, emb_width), jnp.float32)
    )
    layer_rows = (
        lax.psum_scatter(
            user_layer_term.astype(jnp.bfloat16), "table", scatter_dimension=0, tiled=True
        ).astype(jnp.float32),
        lax.psum_scatter(
            user_head_term.astype(jnp.bfloat16), "table", scatter_dimension=0, tiled=True
        ).astype(jnp.float32),
        lax.psum_scatter(
            item_layer_term.astype(jnp.bfloat16), "table", scatter_dimension=0, tiled=True
        ).astype(jnp.float32),
        lax.psum_scatter(
            item_head_term.astype(jnp.bfloat16), "table", scatter_dimension=0, tiled=True
        ).astype(jnp.float32),
    )
    totals = (
        lax.psum(table_part.astype(jnp.bfloat16), "dp").astype(jnp.float32),
        lax.psum(layer_rows[0].astype(jnp.bfloat16), "dp").astype(jnp.float32),
        lax.psum(layer_rows[1].astype(jnp.bfloat16), "dp").astype(jnp.float32),
        lax.psum(layer_rows[2].astype(jnp.bfloat16), "dp").astype(jnp.float32),
        lax.psum(layer_rows[3].astype(jnp.bfloat16), "dp").astype(jnp.float32),
    )
    return (losses, totals[0], totals[1], totals[2], totals[3], totals[4])


BF16 = jnp.bfloat16
F32 = jnp.float32
ROW_ID = jnp.int16
CHUNKS = 4
MESH = pl.DeviceIdType.MESH


def flip(value, mask, bits):
    out = 0
    for bit in range(bits):
        one = lax.rem(lax.div(value, 1 << bit), 2)
        if (mask >> bit) & 1:
            one = 1 - one
        out = out + one * (1 << bit)
    return out


def dot_nt(left, right):
    return lax.dot_general(left, right, (((1,), (1,)), ((), ())), preferred_element_type=F32)


def dot_tn(left, right):
    return lax.dot_general(left, right, (((0,), (0,)), ((), ())), preferred_element_type=F32)


def step_kernel(
    ids_hbm,
    mults_hbm,
    table_hbm,
    user_layer_hbm,
    user_head_hbm,
    item_layer_hbm,
    item_head_hbm,
    counts_hbm,
    losses_ref,
    tower_all,
    table_all,
    ids_ref,
    mults_ref,
    table_ref,
    user_layer_ref,
    user_head_ref,
    item_layer_ref,
    item_head_ref,
    counts_ref,
    user_layer_t,
    user_head_t,
    item_layer_t,
    item_head_t,
    ids_t,
    mults_t,
    table_t,
    row_ids,
    weights,
    parts,
    pair_in,
    sums,
    sums_in,
    slices,
    slices_in,
    units,
    grads,
    tower_terms,
    tower_in,
    tower_mid,
    tower_second,
    table_terms,
    table_in,
    table_mid,
    table_second,
    load_sems,
    pair_sems,
    sums_sems,
    slices_sems,
    units_sems,
    grads_sems,
    pass_sems,
    tower_sems,
    tower_all_sems,
    table_sems,
    table_all_sems,
):
    pairs = (
        (ids_hbm, ids_ref),
        (mults_hbm, mults_ref),
        (table_hbm, table_ref),
        (user_layer_hbm, user_layer_ref),
        (item_layer_hbm, item_layer_ref),
        (user_head_hbm, user_head_ref),
        (item_head_hbm, item_head_ref),
        (counts_hbm, counts_ref),
    )
    loads = [pltpu.make_async_copy(a, b, load_sems.at[i]) for i, (a, b) in enumerate(pairs)]
    for load in loads:
        load.start()
    t = lax.axis_index("table")
    d = lax.axis_index("dp")
    z = lax.div(t, 2)
    core = lax.rem(t, 2)
    sibling = z * 2 + (1 - core)
    z_peers = [flip(z, k, 2) for k in range(4)]
    dp_peers = [flip(d, k, 2) for k in range(4)]

    barrier = pltpu.get_barrier_semaphore()
    for k in range(1, 8):
        pl.semaphore_signal(barrier, inc=1, device_id={"table": flip(t, k, 3)}, device_id_type=MESH)
    for k in range(1, 4):
        pl.semaphore_signal(barrier, inc=1, device_id={"dp": dp_peers[k]}, device_id_type=MESH)

    def send(src, dst, sems, index, target):
        copy = pltpu.make_async_remote_copy(
            src_ref=src,
            dst_ref=dst,
            send_sem=sems.at[0, index],
            recv_sem=sems.at[1, index],
            device_id=target,
            device_id_type=MESH,
        )
        copy.start()
        return copy

    row_ids[...] = lax.broadcasted_iota(jnp.int32, row_ids.shape, 0).astype(row_ids.dtype)
    for load in loads[:3]:
        load.wait()
    ids_t[...] = ids_ref[...].T
    mults_t[...] = mults_ref[...].T
    table_t[...] = table_ref[...].T
    block = 256

    def build_weights(feature):
        id_rows = ids_t[feature * 8 : feature * 8 + 8, :]
        mult_rows = mults_t[feature * 8 : feature * 8 + 8, :].astype(F32)
        spread = [
            (
                jnp.broadcast_to(id_rows[l : l + 1, :], (16, 128)).astype(row_ids.dtype),
                jnp.broadcast_to(mult_rows[l : l + 1, :], (16, 128)).astype(BF16),
            )
            for l in range(LOOKUPS)
        ]
        for start in range(0, 1024, block):
            here = row_ids[start : start + block, :].reshape(block // 16, 16, 128)
            total = None
            for id_row, mult_row in spread:
                term = jnp.where(here == id_row[None], mult_row[None], jnp.zeros((), BF16))
                total = term if total is None else total + term
            weights[start : start + block, feature * 128 : feature * 128 + 128] = total.reshape(
                block, 128
            )

    def pool_pair(pair):
        chunk, first = pair // 2, pair % 2 * 2
        pooled_t = jnp.dot(
            table_t[...], weights[:, pair * 256 : pair * 256 + 256], preferred_element_type=F32
        )
        for half in range(2):
            pooled = pooled_t[:, half * 128 : half * 128 + 128].T.astype(BF16)
            lanes = slice((first + half) * 128, (first + half) * 128 + 128)
            for owner in range(8):
                parts[chunk, owner % 2, owner // 2, :, lanes] = pooled[owner * 16 : owner * 16 + 16]

    pair_copies, sums_copies = [], []

    def pass_on(chunk):
        pair_copies[chunk].wait_recv()
        total = parts[chunk, core].astype(F32) + pair_in[chunk].astype(F32)
        sums[chunk] = total.astype(BF16)
        for k in range(1, 4):
            sums_copies.append(
                send(
                    sums.at[chunk, z_peers[k]],
                    sums_in.at[chunk, k - 1],
                    sums_sems,
                    chunk * 3 + k - 1,
                    {"table": z_peers[k] * 2 + core},
                )
            )

    def pooled_chunk(chunk):
        total = sums[chunk, z].astype(F32)
        for k in range(3):
            sums_copies[chunk * 3 + k].wait_recv()
            total = total + sums_in[chunk, k].astype(F32)
        return total.astype(BF16)

    def tower_out(pre, head):
        hidden = jax.nn.silu(pre).astype(BF16)
        output = jnp.dot(hidden, head, preferred_element_type=F32)
        scale = lax.rsqrt(jnp.sum(output * output, axis=-1, keepdims=True) + EPSILON)
        return hidden, output * scale, scale

    build_weights(0)
    build_weights(1)
    for pair in range(8):
        pool_pair(pair)
        if pair < 7:
            build_weights(pair * 2 + 2)
            build_weights(pair * 2 + 3)
        if pair % 2 == 0:
            continue
        chunk = pair // 2
        if chunk == 0:
            pl.semaphore_wait(barrier, 10)
        pair_copies.append(
            send(
                parts.at[chunk, 1 - core],
                pair_in.at[chunk],
                pair_sems,
                chunk,
                {"table": sibling},
            )
        )
        if chunk > 0:
            pass_on(chunk - 1)
    for load in loads[3:]:
        load.wait()

    user_in = jnp.concatenate([pooled_chunk(0), pooled_chunk(1)], axis=1)
    user_pre = jnp.dot(user_in, user_layer_ref[...], preferred_element_type=F32)
    pass_on(CHUNKS - 1)
    user_hidden, user_unit, user_scale = tower_out(user_pre, user_head_ref[...])
    user_head_t[...] = user_head_ref[...].T
    item_head_t[...] = item_head_ref[...].T
    item_first = pooled_chunk(2)
    item_pre = jnp.dot(item_first, item_layer_ref[0:512, :], preferred_element_type=F32)
    item_last = pooled_chunk(3)
    item_in = jnp.concatenate([item_first, item_last], axis=1)
    item_pre = item_pre + jnp.dot(
        item_last, item_layer_ref[512:1024, :], preferred_element_type=F32
    )
    item_hidden, item_unit, item_scale = tower_out(item_pre, item_head_ref[...])
    eye16 = lax.broadcasted_iota(jnp.int32, (16, 16), 0) == lax.broadcasted_iota(
        jnp.int32, (16, 16), 1
    )
    count_column = jnp.sum(
        jnp.where(eye16, jnp.broadcast_to(counts_ref[...].astype(F32), (16, 16)), 0.0),
        axis=1,
        keepdims=True,
    )
    units[0, :, 0:128] = user_unit.astype(BF16)
    units[0, :, 128:256] = item_unit.astype(BF16)
    units[0, :, 256:384] = jnp.broadcast_to(count_column, (16, 128)).astype(BF16)
    units_copies = [
        send(units.at[0], units.at[k], units_sems, k - 1, {"dp": dp_peers[k]}) for k in range(1, 4)
    ]
    for owner in range(8):
        slices[owner, :, 0:128] = user_in[:, owner * 128 : owner * 128 + 128]
        slices[owner, :, 128:256] = item_in[:, owner * 128 : owner * 128 + 128]
        slices[owner, :, 256:384] = jnp.concatenate(
            [
                user_hidden[:, owner * 64 : owner * 64 + 64],
                item_hidden[:, owner * 64 : owner * 64 + 64],
            ],
            axis=1,
        )
    slices_copies = []
    for k in range(1, 8):
        peer = flip(t, k, 3)
        slices_copies.append(
            send(slices.at[peer], slices_in.at[t], slices_sems, k - 1, {"table": peer})
        )
    slices_in[t] = slices[t]
    for copy in units_copies:
        copy.wait_recv()

    every = units[...]
    users = every[:, :, 0:128].reshape(64, 128)
    items = every[:, :, 128:256].reshape(64, 128)
    log_freq = jnp.log(every[:, :, 256:384].reshape(64, 128).astype(F32))[:, 0:1]
    scores = INVERSE_TEMP * dot_nt(items, users) - log_freq
    lse = jnp.log(jnp.sum(jnp.exp(scores), axis=0, keepdims=True))
    same = lax.broadcasted_iota(jnp.int32, (64, 64), 0) == lax.broadcasted_iota(
        jnp.int32, (64, 64), 1
    )
    positive = jnp.sum(jnp.where(same, scores, 0.0), axis=0, keepdims=True)
    losses_ref[...] = (lse - positive)[:, 0:16]
    dscore = (jnp.exp(scores - lse) - jnp.where(same, 1.0, 0.0)).astype(BF16)
    d_user = INVERSE_TEMP * dot_tn(dscore, items)[0:16]
    d_item = INVERSE_TEMP * jnp.dot(dscore[0:16], users, preferred_element_type=F32)

    def back(d_unit, unit, scale, pre, head_t):
        along = jnp.sum(unit * d_unit, axis=-1, keepdims=True)
        d_output = ((d_unit - unit * along) * scale).astype(BF16)
        d_hidden = (
            jnp.dot(d_output, head_t[...], preferred_element_type=F32) * silu_slope(pre)
        ).astype(BF16)
        return d_output, d_hidden

    user_dout, user_dhid = back(d_user, user_unit, user_scale, user_pre, user_head_t)
    item_dout, item_dhid = back(d_item, item_unit, item_scale, item_pre, item_head_t)
    grads[t] = jnp.concatenate([user_dhid, item_dhid, user_dout, item_dout], axis=1)
    grads_copies = [
        send(
            grads.at[t], grads.at[t], grads_sems, k - 1, {"table": z_peers[k] * 2 + core}
        )
        for k in range(1, 4)
    ]
    pass_copies = [send(grads.at[t], grads.at[t], pass_sems, 0, {"table": sibling})]
    user_layer_t[...] = user_layer_ref[...].T
    item_layer_t[...] = item_layer_ref[...].T
    for k in range(1, 4):
        grads_copies[k - 1].wait_recv()
        slot = z_peers[k] * 2 + core
        pass_copies.append(
            send(grads.at[slot], grads.at[slot], pass_sems, k, {"table": sibling})
        )
    for copy in pass_copies:
        copy.wait_recv()
    for copy in slices_copies:
        copy.wait_recv()

    every = grads[...].reshape(128, 1280)
    kept = slices_in[...].reshape(128, 384)
    user_rows = dot_tn(kept[:, 0:128], every[:, 0:512]).astype(BF16)
    item_rows = dot_tn(kept[:, 128:256], every[:, 512:1024]).astype(BF16)
    head_rows = dot_tn(kept[:, 256:384], every[:, 1024:1280]).astype(BF16)
    for part in range(4):
        lanes = slice(part * 128, part * 128 + 128)
        tower_terms[part, 0, 0:128, :] = user_rows[:, lanes]
        tower_terms[part, 0, 128:144, :] = head_rows[part * 16 : part * 16 + 16, 0:128]
        tower_terms[part, 1, 0:128, :] = item_rows[:, lanes]
        tower_terms[part, 1, 128:144, :] = head_rows[64 + part * 16 : 80 + part * 16, 128:256]

    by_x, by_y, across = dp_peers[1], dp_peers[2], dp_peers[3]

    def scatter_start(terms, first, sems):
        return [
            send(terms.at[across, 0], first.at[0, 1], sems, 0, {"dp": by_x}),
            send(terms.at[across, 1], first.at[1, 1], sems, 1, {"dp": by_y}),
            send(terms.at[by_x, 0], first.at[0, 0], sems, 2, {"dp": by_x}),
            send(terms.at[by_y, 1], first.at[1, 0], sems, 3, {"dp": by_y}),
        ]

    def scatter_pass(terms, first, middle, second, copies, sems):
        for half, target in ((0, by_y), (1, by_x)):
            copies[half].wait_recv()
            total = terms[target, half].astype(F32) + first[half, 1].astype(F32)
            middle[half] = total.astype(BF16)
            copies.append(
                send(middle.at[half], second.at[half], sems, 4 + half, {"dp": target})
            )

    def gather_start(terms, first, second, copies, result, sems):
        for half in range(2):
            copies[2 + half].wait_recv()
            copies[4 + half].wait_recv()
            total = terms[d, half].astype(F32) + first[half, 0].astype(F32)
            result[d, half] = (total + second[half].astype(F32)).astype(BF16)
        own = [result.at[d, 0], result.at[d, 1]]
        return [
            send(own[0], own[0], sems, 0, {"dp": by_y}),
            send(own[1], own[1], sems, 1, {"dp": by_x}),
            send(own[0], own[0], sems, 2, {"dp": by_x}),
            send(own[1], own[1], sems, 3, {"dp": by_y}),
        ]

    def gather_pass(copies, result, sems):
        for half, source, target in ((0, by_y, by_x), (1, by_x, by_y)):
            copies[half].wait_recv()
            held = result.at[source, half]
            copies.append(send(held, held, sems, 4 + half, {"dp": target}))

    tower_copies = scatter_start(tower_terms, tower_in, tower_sems)

    user_dpool = jnp.dot(
        every[:, 0:512], user_layer_t[...], preferred_element_type=F32
    ).astype(BF16)
    item_dpool = jnp.dot(
        every[:, 512:1024], item_layer_t[...], preferred_element_type=F32
    ).astype(BF16)
    columns = [user_dpool[:, f * 128 : f * 128 + 128] for f in range(8)] + [
        item_dpool[:, f * 128 : f * 128 + 128] for f in range(8)
    ]
    d_pooled = jnp.concatenate(columns, axis=0)
    for part in range(4):
        table_terms[part] = (
            jnp.dot(
                weights[part * 256 : part * 256 + 256, :], d_pooled, preferred_element_type=F32
            )
            .astype(BF16)
            .reshape(2, 128, 128)
        )
    table_copies = scatter_start(table_terms, table_in, table_sems)
    scatter_pass(tower_terms, tower_in, tower_mid, tower_second, tower_copies, tower_sems)
    scatter_pass(table_terms, table_in, table_mid, table_second, table_copies, table_sems)
    tower_all_copies = gather_start(
        tower_terms, tower_in, tower_second, tower_copies, tower_all, tower_all_sems
    )
    table_all_copies = gather_start(
        table_terms, table_in, table_second, table_copies, table_all, table_all_sems
    )
    gather_pass(tower_all_copies, tower_all, tower_all_sems)
    gather_pass(table_all_copies, table_all, table_all_sems)
    for copy in tower_all_copies[2:] + table_all_copies[2:]:
        copy.wait_recv()
    for copy in (
        pair_copies
        + sums_copies
        + units_copies
        + slices_copies
        + grads_copies
        + pass_copies
        + tower_copies
        + table_copies
        + tower_all_copies
        + table_all_copies
    ):
        copy.wait_send()


def finish_kernel(
    losses_ref,
    tower_ref,
    table_ref,
    losses_out,
    table_out,
    user_layer_out,
    user_head_out,
    item_layer_out,
    item_head_out,
    table_wide,
    user_layer_wide,
    user_head_wide,
    item_layer_wide,
    item_head_wide,
    sems,
):
    copies = []

    def put(src, dst):
        copies.append(pltpu.make_async_copy(src, dst, sems.at[len(copies)]))
        copies[-1].start()

    put(losses_ref, losses_out)
    for part in range(4):
        table_wide[part * 256 : part * 256 + 256, :] = table_ref[part].reshape(256, 128).astype(F32)
    put(table_wide, table_out)
    for part in range(4):
        lanes = slice(part * 128, part * 128 + 128)
        user_layer_wide[:, lanes] = tower_ref[part, 0, 0:128, :].astype(F32)
    put(user_layer_wide, user_layer_out)
    for part in range(4):
        lanes = slice(part * 128, part * 128 + 128)
        item_layer_wide[:, lanes] = tower_ref[part, 1, 0:128, :].astype(F32)
    put(item_layer_wide, item_layer_out)
    for part in range(4):
        rows = slice(part * 16, part * 16 + 16)
        user_head_wide[rows, :] = tower_ref[part, 0, 128:144, :].astype(F32)
        item_head_wide[rows, :] = tower_ref[part, 1, 128:144, :].astype(F32)
    put(user_head_wide, user_head_out)
    put(item_head_wide, item_head_out)
    for copy in copies:
        copy.wait()


def shards(ids, mults, table, user_layer, user_head, item_layer, item_head, counts):
    small = lax.axis_size("table") == 8 and lax.axis_size("dp") == 4
    if not small or ids.shape != (1, 128, 128) or table.shape != (1024, 128):
        return shards_general(
            ids, mults, table, user_layer, user_head, item_layer, item_head, counts
        )

    def dma(count):
        return pltpu.SemaphoreType.DMA((2, count))

    held = [
        pltpu.with_memory_space_constraint(x, pltpu.HBM)
        for x in (ids[0], mults[0], table, user_layer, user_head, item_layer, item_head, counts)
    ]
    vmem = pl.BlockSpec(memory_space=pltpu.VMEM)
    hbm = pl.BlockSpec(memory_space=pltpu.HBM)
    losses, tower_all, table_all = pl.pallas_call(
        step_kernel,
        out_shape=(
            jax.ShapeDtypeStruct((1, 16), F32),
            jax.ShapeDtypeStruct((4, 2, 144, 128), BF16),
            jax.ShapeDtypeStruct((4, 2, 128, 128), BF16),
        ),
        in_specs=[hbm] * 8,
        out_specs=(vmem,) * 3,
        scratch_shapes=[
            pltpu.VMEM((128, 128), jnp.int32),
            pltpu.VMEM((128, 128), jnp.int32),
            pltpu.VMEM((1024, 128), BF16),
            pltpu.VMEM((1024, 512), BF16),
            pltpu.VMEM((512, 128), BF16),
            pltpu.VMEM((1024, 512), BF16),
            pltpu.VMEM((512, 128), BF16),
            pltpu.VMEM((1, 16), jnp.int32),
            pltpu.VMEM((512, 1024), BF16),
            pltpu.VMEM((128, 512), BF16),
            pltpu.VMEM((512, 1024), BF16),
            pltpu.VMEM((128, 512), BF16),
            pltpu.VMEM((128, 128), jnp.int32),
            pltpu.VMEM((128, 128), jnp.int32),
            pltpu.VMEM((128, 1024), BF16),
            pltpu.VMEM((1024, 128), ROW_ID),
            pltpu.VMEM((1024, 2048), BF16),
            pltpu.VMEM((CHUNKS, 2, 4, 16, 512), BF16),
            pltpu.VMEM((CHUNKS, 4, 16, 512), BF16),
            pltpu.VMEM((CHUNKS, 4, 16, 512), BF16),
            pltpu.VMEM((CHUNKS, 3, 16, 512), BF16),
            pltpu.VMEM((8, 16, 384), BF16),
            pltpu.VMEM((8, 16, 384), BF16),
            pltpu.VMEM((4, 16, 384), BF16),
            pltpu.VMEM((8, 16, 1280), BF16),
            pltpu.VMEM((4, 2, 144, 128), BF16),
            pltpu.VMEM((2, 2, 144, 128), BF16),
            pltpu.VMEM((2, 144, 128), BF16),
            pltpu.VMEM((2, 144, 128), BF16),
            pltpu.VMEM((4, 2, 128, 128), BF16),
            pltpu.VMEM((2, 2, 128, 128), BF16),
            pltpu.VMEM((2, 128, 128), BF16),
            pltpu.VMEM((2, 128, 128), BF16),
            pltpu.SemaphoreType.DMA((8,)),
            dma(CHUNKS),
            dma(CHUNKS * 3),
            dma(7),
            dma(3),
            dma(3),
            dma(4),
            dma(6),
            dma(6),
            dma(6),
            dma(6),
        ],
        compiler_params=pltpu.CompilerParams(
            collective_id=0, has_side_effects=True, vmem_limit_bytes=40 * 1024 * 1024
        ),
        cost_estimate=pl.CostEstimate(
            flops=3_000_000_000, bytes_accessed=4_500_000, transcendentals=100_000
        ),
    )(*held)
    return pl.pallas_call(
        finish_kernel,
        out_shape=(
            jax.ShapeDtypeStruct((1, 16), F32),
            jax.ShapeDtypeStruct((1024, 128), F32),
            jax.ShapeDtypeStruct((128, 512), F32),
            jax.ShapeDtypeStruct((64, 128), F32),
            jax.ShapeDtypeStruct((128, 512), F32),
            jax.ShapeDtypeStruct((64, 128), F32),
        ),
        in_specs=[vmem] * 3,
        out_specs=(hbm,) * 6,
        scratch_shapes=[
            pltpu.VMEM((1024, 128), F32),
            pltpu.VMEM((128, 512), F32),
            pltpu.VMEM((64, 128), F32),
            pltpu.VMEM((128, 512), F32),
            pltpu.VMEM((64, 128), F32),
            pltpu.SemaphoreType.DMA((6,)),
        ],
        compiler_params=pltpu.CompilerParams(vmem_limit_bytes=16 * 1024 * 1024),
    )(losses, tower_all, table_all)


def solution(mesh):
    in_specs = (
        P("table", "dp", None),
        P("table", "dp", None),
        P("table", None),
        P(),
        P(),
        P(),
        P(),
        P("dp", "table"),
    )
    out_specs = (
        P("dp", "table"),
        P("table", None),
        P("table", None),
        P("table", None),
        P("table", None),
        P("table", None),
    )
    return jax.shard_map(shards, mesh=mesh, in_specs=in_specs, out_specs=out_specs, check_vma=False)
```

```python
import functools

import jax
import jax.numpy as jnp
from jax import lax
from jax.experimental import pallas as pl
from jax.experimental.pallas import tpu as pltpu
from jax.sharding import PartitionSpec as P

LOOKUPS = 8


INVERSE_TEMP = 20.0
EPSILON = 1e-06


def silu_slope(pre):
    gate = jax.nn.sigmoid(pre)
    return gate * (1.0 + pre * (1.0 - gate))


def run_tower(pooled_in, layer, head):
    pre = jnp.dot(pooled_in, layer, preferred_element_type=jnp.float32)
    hidden = jax.nn.silu(pre).astype(jnp.bfloat16)
    output = jnp.dot(hidden, head, preferred_element_type=jnp.float32)
    scale = lax.rsqrt(jnp.sum(output * output, axis=-1, keepdims=True) + EPSILON)
    return (pre, hidden, output * scale, scale)


def tower_back(d_unit, unit, scale, pre, hidden, pooled_in, head):
    along = jnp.sum(unit * d_unit, axis=-1, keepdims=True)
    d_output = ((d_unit - unit * along) * scale).astype(jnp.bfloat16)
    back = lax.dot_general(
        d_output, head, (((1,), (1,)), ((), ())), preferred_element_type=jnp.float32
    )
    d_hidden = (back * silu_slope(pre)).astype(jnp.bfloat16)
    layer_term = lax.dot_general(
        pooled_in, d_hidden, (((0,), (0,)), ((), ())), preferred_element_type=jnp.float32
    )
    head_term = lax.dot_general(
        hidden, d_output, (((0,), (0,)), ((), ())), preferred_element_type=jnp.float32
    )
    return (d_output, d_hidden, layer_term, head_term)


def input_grads(d_hidden, layer):
    return lax.dot_general(
        d_hidden, layer, (((1,), (1,)), ((), ())), preferred_element_type=jnp.float32
    ).astype(jnp.bfloat16)


def shards_general(ids, mults, table, user_layer, user_head, item_layer, item_head, counts):
    table_count = lax.axis_size("table")
    rows_dev, emb_width = table.shape
    group_rows = ids.shape[1]
    feature_count = ids.shape[2] // LOOKUPS
    own_rows = group_rows // table_count
    user_width = user_layer.shape[0]
    id_blocks = ids[0].reshape(group_rows, feature_count, LOOKUPS).transpose(1, 0, 2)
    mult_blocks = mults[0].reshape(group_rows, feature_count, LOOKUPS).transpose(1, 0, 2)
    table_rows = lax.broadcasted_iota(jnp.int32, (1, rows_dev), 1)

    def lookup_weights(id_block, mult_block):
        running = jnp.zeros((group_rows, rows_dev), jnp.float32)
        for lookup in range(LOOKUPS):
            hit = id_block[:, lookup : lookup + 1] == table_rows
            running = running + jnp.where(
                hit, mult_block[:, lookup : lookup + 1].astype(jnp.float32), 0.0
            )
        return running.astype(jnp.bfloat16)

    def pool_feature(lookup_pair):
        weights = lookup_weights(lookup_pair[0], lookup_pair[1])
        return jnp.dot(weights, table, preferred_element_type=jnp.float32).astype(jnp.bfloat16)

    partial_value = lax.map(pool_feature, (id_blocks, mult_blocks))
    received = lax.all_to_all(partial_value, "table", split_axis=1, concat_axis=1, tiled=True)
    pooled = jnp.sum(
        received.astype(jnp.float32).reshape(feature_count, table_count, own_rows, emb_width),
        axis=1,
    ).astype(jnp.bfloat16)
    pooled = pooled.transpose(1, 0, 2).reshape(own_rows, feature_count * emb_width)
    user_in = pooled[:, :user_width]
    item_in = pooled[:, user_width:]
    user_pre, user_hidden, user_unit, user_scale = run_tower(user_in, user_layer, user_head)
    item_pre, item_hidden, item_unit, item_scale = run_tower(item_in, item_layer, item_head)
    user_vector = user_unit.astype(jnp.bfloat16)
    item_vector = item_unit.astype(jnp.bfloat16)
    item_rows, item_counts = (
        lax.all_gather(item_vector, "dp", axis=0, tiled=True),
        lax.all_gather(counts[0].astype(jnp.bfloat16), "dp", axis=0, tiled=True),
    )
    log_freq = jnp.log(item_counts.astype(jnp.float32))
    scores = (
        INVERSE_TEMP
        * lax.dot_general(
            user_vector, item_rows, (((1,), (1,)), ((), ())), preferred_element_type=jnp.float32
        )
        - log_freq[None, :]
    )
    lse = jnp.log(jnp.sum(jnp.exp(scores), axis=-1))
    own_index = lax.axis_index("dp") * own_rows + lax.broadcasted_iota(jnp.int32, (own_rows,), 0)
    columns = lax.broadcasted_iota(jnp.int32, scores.shape, 1)
    is_positive = columns == own_index[:, None]
    positive = jnp.sum(jnp.where(is_positive, scores, 0.0), axis=-1)
    losses = (lse - positive)[None, :]
    dscore = (jnp.exp(scores - lse[:, None]) - is_positive.astype(jnp.float32)).astype(jnp.bfloat16)
    d_user = INVERSE_TEMP * jnp.dot(dscore, item_rows, preferred_element_type=jnp.float32)
    item_terms = INVERSE_TEMP * lax.dot_general(
        dscore, user_vector, (((0,), (0,)), ((), ())), preferred_element_type=jnp.float32
    )
    d_item = lax.psum_scatter(
        item_terms.astype(jnp.bfloat16), "dp", scatter_dimension=0, tiled=True
    ).astype(jnp.float32)
    user_dout, user_dhid, user_layer_term, user_head_term = tower_back(
        d_user, user_unit, user_scale, user_pre, user_hidden, user_in, user_head
    )
    item_dout, item_dhid, item_layer_term, item_head_term = tower_back(
        d_item, item_unit, item_scale, item_pre, item_hidden, item_in, item_head
    )
    own_grads = jnp.concatenate(
        [input_grads(user_dhid, user_layer), input_grads(item_dhid, item_layer)], axis=1
    )
    group_grads = lax.all_gather(own_grads, "table", axis=0, tiled=True)

    def add_feature(feature, running):
        weights = lookup_weights(id_blocks[feature], mult_blocks[feature])
        column = lax.dynamic_slice_in_dim(group_grads, feature * emb_width, emb_width, 1)
        return running + lax.dot_general(
            weights, column, (((0,), (0,)), ((), ())), preferred_element_type=jnp.float32
        )

    table_part = lax.fori_loop(
        0, feature_count, add_feature, jnp.zeros((rows_dev, emb_width), jnp.float32)
    )
    layer_rows = (
        lax.psum_scatter(
            user_layer_term.astype(jnp.bfloat16), "table", scatter_dimension=0, tiled=True
        ).astype(jnp.float32),
        lax.psum_scatter(
            user_head_term.astype(jnp.bfloat16), "table", scatter_dimension=0, tiled=True
        ).astype(jnp.float32),
        lax.psum_scatter(
            item_layer_term.astype(jnp.bfloat16), "table", scatter_dimension=0, tiled=True
        ).astype(jnp.float32),
        lax.psum_scatter(
            item_head_term.astype(jnp.bfloat16), "table", scatter_dimension=0, tiled=True
        ).astype(jnp.float32),
    )
    totals = (
        lax.psum(table_part.astype(jnp.bfloat16), "dp").astype(jnp.float32),
        lax.psum(layer_rows[0].astype(jnp.bfloat16), "dp").astype(jnp.float32),
        lax.psum(layer_rows[1].astype(jnp.bfloat16), "dp").astype(jnp.float32),
        lax.psum(layer_rows[2].astype(jnp.bfloat16), "dp").astype(jnp.float32),
        lax.psum(layer_rows[3].astype(jnp.bfloat16), "dp").astype(jnp.float32),
    )
    return (losses, totals[0], totals[1], totals[2], totals[3], totals[4])


BF16 = jnp.bfloat16
F32 = jnp.float32
ROW_ID = jnp.int16
CHUNKS = 4
MESH = pl.DeviceIdType.MESH


def flip(value, mask, bits):
    out = 0
    for bit in range(bits):
        one = lax.rem(lax.div(value, 1 << bit), 2)
        if (mask >> bit) & 1:
            one = 1 - one
        out = out + one * (1 << bit)
    return out


def dot_nt(left, right):
    return lax.dot_general(left, right, (((1,), (1,)), ((), ())), preferred_element_type=F32)


def dot_tn(left, right):
    return lax.dot_general(left, right, (((0,), (0,)), ((), ())), preferred_element_type=F32)


def step_kernel(
    ids_hbm,
    mults_hbm,
    table_hbm,
    user_layer_hbm,
    user_head_hbm,
    item_layer_hbm,
    item_head_hbm,
    counts_hbm,
    losses_ref,
    tower_all,
    table_all,
    ids_ref,
    mults_ref,
    table_ref,
    user_layer_ref,
    user_head_ref,
    item_layer_ref,
    item_head_ref,
    counts_ref,
    user_layer_t,
    user_head_t,
    item_layer_t,
    item_head_t,
    ids_t,
    mults_t,
    table_t,
    row_ids,
    weights,
    parts,
    pair_in,
    sums,
    sums_in,
    slices,
    slices_in,
    units,
    grads,
    tower_terms,
    tower_in,
    tower_mid,
    tower_second,
    table_terms,
    table_in,
    table_mid,
    table_second,
    pooled_grads,
    load_sems,
    pair_sems,
    sums_sems,
    slices_sems,
    units_sems,
    grads_sems,
    pass_sems,
    tower_sems,
    tower_all_sems,
    table_sems,
    table_all_sems,
):
    pairs = (
        (ids_hbm, ids_ref),
        (mults_hbm, mults_ref),
        (table_hbm, table_ref),
        (user_layer_hbm, user_layer_ref),
        (item_layer_hbm, item_layer_ref),
        (user_head_hbm, user_head_ref),
        (item_head_hbm, item_head_ref),
        (counts_hbm, counts_ref),
    )
    loads = [pltpu.make_async_copy(a, b, load_sems.at[i]) for i, (a, b) in enumerate(pairs)]
    for load in loads:
        load.start()
    t = lax.axis_index("table")
    d = lax.axis_index("dp")
    z = lax.div(t, 2)
    core = lax.rem(t, 2)
    sibling = z * 2 + (1 - core)
    z_peers = [flip(z, k, 2) for k in range(4)]
    dp_peers = [flip(d, k, 2) for k in range(4)]

    barrier = pltpu.get_barrier_semaphore()
    for k in range(1, 8):
        pl.semaphore_signal(barrier, inc=1, device_id={"table": flip(t, k, 3)}, device_id_type=MESH)
    for k in range(1, 4):
        pl.semaphore_signal(barrier, inc=1, device_id={"dp": dp_peers[k]}, device_id_type=MESH)

    def send(src, dst, sems, index, target):
        copy = pltpu.make_async_remote_copy(
            src_ref=src,
            dst_ref=dst,
            send_sem=sems.at[0, index],
            recv_sem=sems.at[1, index],
            device_id=target,
            device_id_type=MESH,
        )
        copy.start()
        return copy

    row_ids[...] = lax.broadcasted_iota(jnp.int32, row_ids.shape, 0).astype(row_ids.dtype)
    for load in loads[:3]:
        load.wait()
    ids_t[...] = ids_ref[...].T
    mults_t[...] = mults_ref[...].T
    table_t[...] = table_ref[...].T
    block = 256

    def build_weights(feature):
        slots = pl.ds(pl.multiple_of(feature * 8, 8), 8)
        lanes = pl.ds(pl.multiple_of(feature * 128, 128), 128)
        id_rows = ids_t[slots, :]
        mult_rows = mults_t[slots, :].astype(F32)
        spread = [
            (
                jnp.broadcast_to(id_rows[l : l + 1, :], (16, 128)).astype(row_ids.dtype),
                jnp.broadcast_to(mult_rows[l : l + 1, :], (16, 128)).astype(BF16),
            )
            for l in range(LOOKUPS)
        ]

        def block_step(part, carry):
            rows = pl.ds(pl.multiple_of(part * block, block), block)
            here = row_ids[rows, :].reshape(block // 16, 16, 128)
            total = None
            for id_row, mult_row in spread:
                term = jnp.where(here == id_row[None], mult_row[None], jnp.zeros((), BF16))
                total = term if total is None else total + term
            weights[rows, lanes] = total.reshape(block, 128)
            return carry

        lax.fori_loop(0, 1024 // block, block_step, 0)

    def pool_chunk(chunk):
        lanes = pl.ds(pl.multiple_of(chunk * 512, 512), 512)
        pooled_t = jnp.dot(table_t[...], weights[:, lanes], preferred_element_type=F32)
        for at in range(4):
            pooled = pooled_t[:, at * 128 : at * 128 + 128].T.astype(BF16)
            for owner in range(8):
                parts[chunk, owner % 2, owner // 2, :, at * 128 : at * 128 + 128] = pooled[
                    owner * 16 : owner * 16 + 16
                ]

    def remote(src, dst, sems, index, target):
        return pltpu.make_async_remote_copy(
            src_ref=src,
            dst_ref=dst,
            send_sem=sems.at[0, index],
            recv_sem=sems.at[1, index],
            device_id=target,
            device_id_type=MESH,
        )

    def pair_copy(chunk):
        return remote(
            parts.at[chunk, 1 - core], pair_in.at[chunk], pair_sems, chunk, {"table": sibling}
        )

    def sums_copy(chunk, k):
        return remote(
            sums.at[chunk, z_peers[k]],
            sums_in.at[chunk, k - 1],
            sums_sems,
            chunk * 3 + k - 1,
            {"table": z_peers[k] * 2 + core},
        )

    def pass_on(chunk):
        pair_copy(chunk).wait_recv()
        total = parts[chunk, core].astype(F32) + pair_in[chunk].astype(F32)
        sums[chunk] = total.astype(BF16)
        for k in range(1, 4):
            sums_copy(chunk, k).start()

    def pooled_chunk(chunk):
        total = sums[chunk, z].astype(F32)
        for k in range(3):
            sums_copy(chunk, k + 1).wait_recv()
            total = total + sums_in[chunk, k].astype(F32)
        return total.astype(BF16)

    def tower_out(pre, head):
        hidden = jax.nn.silu(pre).astype(BF16)
        output = jnp.dot(hidden, head, preferred_element_type=F32)
        scale = lax.rsqrt(jnp.sum(output * output, axis=-1, keepdims=True) + EPSILON)
        return hidden, output * scale, scale

    pl.semaphore_wait(barrier, 10)

    def chunk_step(chunk, carry):
        def feature_step(at, inner):
            build_weights(chunk * 4 + at)
            return inner

        lax.fori_loop(0, 4, feature_step, 0)
        pool_chunk(chunk)
        pair_copy(chunk).start()

        @pl.when(chunk > 0)
        def _():
            pass_on(chunk - 1)

        return carry

    lax.fori_loop(0, CHUNKS, chunk_step, 0)
    for load in loads[3:]:
        load.wait()

    user_in = jnp.concatenate([pooled_chunk(0), pooled_chunk(1)], axis=1)
    user_pre = jnp.dot(user_in, user_layer_ref[...], preferred_element_type=F32)
    pass_on(CHUNKS - 1)
    user_hidden, user_unit, user_scale = tower_out(user_pre, user_head_ref[...])
    user_head_t[...] = user_head_ref[...].T
    item_head_t[...] = item_head_ref[...].T
    item_first = pooled_chunk(2)
    item_pre = jnp.dot(item_first, item_layer_ref[0:512, :], preferred_element_type=F32)
    item_last = pooled_chunk(3)
    item_in = jnp.concatenate([item_first, item_last], axis=1)
    item_pre = item_pre + jnp.dot(
        item_last, item_layer_ref[512:1024, :], preferred_element_type=F32
    )
    item_hidden, item_unit, item_scale = tower_out(item_pre, item_head_ref[...])
    eye16 = lax.broadcasted_iota(jnp.int32, (16, 16), 0) == lax.broadcasted_iota(
        jnp.int32, (16, 16), 1
    )
    count_column = jnp.sum(
        jnp.where(eye16, jnp.broadcast_to(counts_ref[...].astype(F32), (16, 16)), 0.0),
        axis=1,
        keepdims=True,
    )
    units[0, :, 0:128] = user_unit.astype(BF16)
    units[0, :, 128:256] = item_unit.astype(BF16)
    units[0, :, 256:384] = jnp.broadcast_to(count_column, (16, 128)).astype(BF16)
    units_copies = [
        send(units.at[0], units.at[k], units_sems, k - 1, {"dp": dp_peers[k]}) for k in range(1, 4)
    ]
    for owner in range(8):
        slices[owner, :, 0:128] = user_in[:, owner * 128 : owner * 128 + 128]
        slices[owner, :, 128:256] = item_in[:, owner * 128 : owner * 128 + 128]
        slices[owner, :, 256:384] = jnp.concatenate(
            [
                user_hidden[:, owner * 64 : owner * 64 + 64],
                item_hidden[:, owner * 64 : owner * 64 + 64],
            ],
            axis=1,
        )
    slices_copies = []
    for k in range(1, 8):
        peer = flip(t, k, 3)
        slices_copies.append(
            send(slices.at[peer], slices_in.at[t], slices_sems, k - 1, {"table": peer})
        )
    slices_in[t] = slices[t]
    for copy in units_copies:
        copy.wait_recv()

    every = units[...]
    users = every[:, :, 0:128].reshape(64, 128)
    items = every[:, :, 128:256].reshape(64, 128)
    log_freq = jnp.log(every[:, :, 256:384].reshape(64, 128).astype(F32))[:, 0:1]
    scores = INVERSE_TEMP * dot_nt(items, users) - log_freq
    lse = jnp.log(jnp.sum(jnp.exp(scores), axis=0, keepdims=True))
    same = lax.broadcasted_iota(jnp.int32, (64, 64), 0) == lax.broadcasted_iota(
        jnp.int32, (64, 64), 1
    )
    positive = jnp.sum(jnp.where(same, scores, 0.0), axis=0, keepdims=True)
    losses_ref[...] = (lse - positive)[:, 0:16]
    dscore = (jnp.exp(scores - lse) - jnp.where(same, 1.0, 0.0)).astype(BF16)
    d_user = INVERSE_TEMP * dot_tn(dscore, items)[0:16]
    d_item = INVERSE_TEMP * jnp.dot(dscore[0:16], users, preferred_element_type=F32)

    def back(d_unit, unit, scale, pre, head_t):
        along = jnp.sum(unit * d_unit, axis=-1, keepdims=True)
        d_output = ((d_unit - unit * along) * scale).astype(BF16)
        d_hidden = (
            jnp.dot(d_output, head_t[...], preferred_element_type=F32) * silu_slope(pre)
        ).astype(BF16)
        return d_output, d_hidden

    user_dout, user_dhid = back(d_user, user_unit, user_scale, user_pre, user_head_t)
    item_dout, item_dhid = back(d_item, item_unit, item_scale, item_pre, item_head_t)
    grads[t] = jnp.concatenate([user_dhid, item_dhid, user_dout, item_dout], axis=1)
    grads_copies = [
        send(
            grads.at[t], grads.at[t], grads_sems, k - 1, {"table": z_peers[k] * 2 + core}
        )
        for k in range(1, 4)
    ]
    pass_copies = [send(grads.at[t], grads.at[t], pass_sems, 0, {"table": sibling})]

    def turn(part, carry):
        rows = pl.ds(pl.multiple_of(part * 128, 128), 128)
        user_layer_t[:, rows] = user_layer_ref[rows, :].T
        item_layer_t[:, rows] = item_layer_ref[rows, :].T
        return carry

    lax.fori_loop(0, 8, turn, 0)
    for k in range(1, 4):
        grads_copies[k - 1].wait_recv()
        slot = z_peers[k] * 2 + core
        pass_copies.append(
            send(grads.at[slot], grads.at[slot], pass_sems, k, {"table": sibling})
        )
    for copy in pass_copies:
        copy.wait_recv()
    for copy in slices_copies:
        copy.wait_recv()

    every = grads[...].reshape(128, 1280)
    kept = slices_in[...].reshape(128, 384)
    user_rows = dot_tn(kept[:, 0:128], every[:, 0:512]).astype(BF16)
    item_rows = dot_tn(kept[:, 128:256], every[:, 512:1024]).astype(BF16)
    head_rows = dot_tn(kept[:, 256:384], every[:, 1024:1280]).astype(BF16)
    for part in range(4):
        lanes = slice(part * 128, part * 128 + 128)
        tower_terms[part, 0, 0:128, :] = user_rows[:, lanes]
        tower_terms[part, 0, 128:144, :] = head_rows[part * 16 : part * 16 + 16, 0:128]
        tower_terms[part, 1, 0:128, :] = item_rows[:, lanes]
        tower_terms[part, 1, 128:144, :] = head_rows[64 + part * 16 : 80 + part * 16, 128:256]

    by_x, by_y, across = dp_peers[1], dp_peers[2], dp_peers[3]

    def scatter_start(terms, first, sems):
        return [
            send(terms.at[across, 0], first.at[0, 1], sems, 0, {"dp": by_x}),
            send(terms.at[across, 1], first.at[1, 1], sems, 1, {"dp": by_y}),
            send(terms.at[by_x, 0], first.at[0, 0], sems, 2, {"dp": by_x}),
            send(terms.at[by_y, 1], first.at[1, 0], sems, 3, {"dp": by_y}),
        ]

    def scatter_pass(terms, first, middle, second, copies, sems):
        for half, target in ((0, by_y), (1, by_x)):
            copies[half].wait_recv()
            total = terms[target, half].astype(F32) + first[half, 1].astype(F32)
            middle[half] = total.astype(BF16)
            copies.append(
                send(middle.at[half], second.at[half], sems, 4 + half, {"dp": target})
            )

    def gather_start(terms, first, second, copies, result, sems):
        for half in range(2):
            copies[2 + half].wait_recv()
            copies[4 + half].wait_recv()
            total = terms[d, half].astype(F32) + first[half, 0].astype(F32)
            result[d, half] = (total + second[half].astype(F32)).astype(BF16)
        own = [result.at[d, 0], result.at[d, 1]]
        return [
            send(own[0], own[0], sems, 0, {"dp": by_y}),
            send(own[1], own[1], sems, 1, {"dp": by_x}),
            send(own[0], own[0], sems, 2, {"dp": by_x}),
            send(own[1], own[1], sems, 3, {"dp": by_y}),
        ]

    def gather_pass(copies, result, sems):
        for half, source, target in ((0, by_y, by_x), (1, by_x, by_y)):
            copies[half].wait_recv()
            held = result.at[source, half]
            copies.append(send(held, held, sems, 4 + half, {"dp": target}))

    tower_copies = scatter_start(tower_terms, tower_in, tower_sems)

    user_dpool = jnp.dot(
        every[:, 0:512], user_layer_t[...], preferred_element_type=F32
    ).astype(BF16)
    item_dpool = jnp.dot(
        every[:, 512:1024], item_layer_t[...], preferred_element_type=F32
    ).astype(BF16)
    columns = [user_dpool[:, f * 128 : f * 128 + 128] for f in range(8)] + [
        item_dpool[:, f * 128 : f * 128 + 128] for f in range(8)
    ]
    d_pooled = jnp.concatenate(columns, axis=0)
    pooled_grads[...] = d_pooled

    def table_step(part, carry):
        rows = pl.ds(pl.multiple_of(part * 512, 512), 512)
        terms = jnp.dot(weights[rows, :], pooled_grads[...], preferred_element_type=F32)
        table_terms[pl.ds(part * 2, 2)] = terms.astype(BF16).reshape(2, 2, 128, 128)
        return carry

    lax.fori_loop(0, 2, table_step, 0)
    table_copies = scatter_start(table_terms, table_in, table_sems)
    scatter_pass(tower_terms, tower_in, tower_mid, tower_second, tower_copies, tower_sems)
    scatter_pass(table_terms, table_in, table_mid, table_second, table_copies, table_sems)
    tower_all_copies = gather_start(
        tower_terms, tower_in, tower_second, tower_copies, tower_all, tower_all_sems
    )
    table_all_copies = gather_start(
        table_terms, table_in, table_second, table_copies, table_all, table_all_sems
    )
    gather_pass(tower_all_copies, tower_all, tower_all_sems)
    gather_pass(table_all_copies, table_all, table_all_sems)
    for copy in tower_all_copies[2:] + table_all_copies[2:]:
        copy.wait_recv()
    for copy in (
        [pair_copy(chunk) for chunk in range(CHUNKS)]
        + [sums_copy(chunk, k) for chunk in range(CHUNKS) for k in range(1, 4)]
        + units_copies
        + slices_copies
        + grads_copies
        + pass_copies
        + tower_copies
        + table_copies
        + tower_all_copies
        + table_all_copies
    ):
        copy.wait_send()


def finish_kernel(
    losses_ref,
    tower_ref,
    table_ref,
    losses_out,
    table_out,
    user_layer_out,
    user_head_out,
    item_layer_out,
    item_head_out,
    table_wide,
    user_layer_wide,
    user_head_wide,
    item_layer_wide,
    item_head_wide,
    sems,
):
    copies = []

    def put(src, dst):
        copies.append(pltpu.make_async_copy(src, dst, sems.at[len(copies)]))
        copies[-1].start()

    put(losses_ref, losses_out)
    for part in range(4):
        table_wide[part * 256 : part * 256 + 256, :] = table_ref[part].reshape(256, 128).astype(F32)
    put(table_wide, table_out)
    for part in range(4):
        lanes = slice(part * 128, part * 128 + 128)
        user_layer_wide[:, lanes] = tower_ref[part, 0, 0:128, :].astype(F32)
    put(user_layer_wide, user_layer_out)
    for part in range(4):
        lanes = slice(part * 128, part * 128 + 128)
        item_layer_wide[:, lanes] = tower_ref[part, 1, 0:128, :].astype(F32)
    put(item_layer_wide, item_layer_out)
    for part in range(4):
        rows = slice(part * 16, part * 16 + 16)
        user_head_wide[rows, :] = tower_ref[part, 0, 128:144, :].astype(F32)
        item_head_wide[rows, :] = tower_ref[part, 1, 128:144, :].astype(F32)
    put(user_head_wide, user_head_out)
    put(item_head_wide, item_head_out)
    for copy in copies:
        copy.wait()


def shards(ids, mults, table, user_layer, user_head, item_layer, item_head, counts):
    small = lax.axis_size("table") == 8 and lax.axis_size("dp") == 4
    if not small or ids.shape != (1, 128, 128) or table.shape != (1024, 128):
        return shards_general(
            ids, mults, table, user_layer, user_head, item_layer, item_head, counts
        )

    def dma(count):
        return pltpu.SemaphoreType.DMA((2, count))

    held = [
        pltpu.with_memory_space_constraint(x, pltpu.HBM)
        for x in (ids[0], mults[0], table, user_layer, user_head, item_layer, item_head, counts)
    ]
    vmem = pl.BlockSpec(memory_space=pltpu.VMEM)
    hbm = pl.BlockSpec(memory_space=pltpu.HBM)
    losses, tower_all, table_all = pl.pallas_call(
        step_kernel,
        out_shape=(
            jax.ShapeDtypeStruct((1, 16), F32),
            jax.ShapeDtypeStruct((4, 2, 144, 128), BF16),
            jax.ShapeDtypeStruct((4, 2, 128, 128), BF16),
        ),
        in_specs=[hbm] * 8,
        out_specs=(vmem,) * 3,
        scratch_shapes=[
            pltpu.VMEM((128, 128), jnp.int32),
            pltpu.VMEM((128, 128), jnp.int32),
            pltpu.VMEM((1024, 128), BF16),
            pltpu.VMEM((1024, 512), BF16),
            pltpu.VMEM((512, 128), BF16),
            pltpu.VMEM((1024, 512), BF16),
            pltpu.VMEM((512, 128), BF16),
            pltpu.VMEM((1, 16), jnp.int32),
            pltpu.VMEM((512, 1024), BF16),
            pltpu.VMEM((128, 512), BF16),
            pltpu.VMEM((512, 1024), BF16),
            pltpu.VMEM((128, 512), BF16),
            pltpu.VMEM((128, 128), jnp.int32),
            pltpu.VMEM((128, 128), jnp.int32),
            pltpu.VMEM((128, 1024), BF16),
            pltpu.VMEM((1024, 128), ROW_ID),
            pltpu.VMEM((1024, 2048), BF16),
            pltpu.VMEM((CHUNKS, 2, 4, 16, 512), BF16),
            pltpu.VMEM((CHUNKS, 4, 16, 512), BF16),
            pltpu.VMEM((CHUNKS, 4, 16, 512), BF16),
            pltpu.VMEM((CHUNKS, 3, 16, 512), BF16),
            pltpu.VMEM((8, 16, 384), BF16),
            pltpu.VMEM((8, 16, 384), BF16),
            pltpu.VMEM((4, 16, 384), BF16),
            pltpu.VMEM((8, 16, 1280), BF16),
            pltpu.VMEM((4, 2, 144, 128), BF16),
            pltpu.VMEM((2, 2, 144, 128), BF16),
            pltpu.VMEM((2, 144, 128), BF16),
            pltpu.VMEM((2, 144, 128), BF16),
            pltpu.VMEM((4, 2, 128, 128), BF16),
            pltpu.VMEM((2, 2, 128, 128), BF16),
            pltpu.VMEM((2, 128, 128), BF16),
            pltpu.VMEM((2, 128, 128), BF16),
            pltpu.VMEM((2048, 128), BF16),
            pltpu.SemaphoreType.DMA((8,)),
            dma(CHUNKS),
            dma(CHUNKS * 3),
            dma(7),
            dma(3),
            dma(3),
            dma(4),
            dma(6),
            dma(6),
            dma(6),
            dma(6),
        ],
        compiler_params=pltpu.CompilerParams(
            collective_id=0, has_side_effects=True, vmem_limit_bytes=40 * 1024 * 1024
        ),
        cost_estimate=pl.CostEstimate(
            flops=3_000_000_000, bytes_accessed=4_500_000, transcendentals=100_000
        ),
    )(*held)
    return pl.pallas_call(
        finish_kernel,
        out_shape=(
            jax.ShapeDtypeStruct((1, 16), F32),
            jax.ShapeDtypeStruct((1024, 128), F32),
            jax.ShapeDtypeStruct((128, 512), F32),
            jax.ShapeDtypeStruct((64, 128), F32),
            jax.ShapeDtypeStruct((128, 512), F32),
            jax.ShapeDtypeStruct((64, 128), F32),
        ),
        in_specs=[vmem] * 3,
        out_specs=(hbm,) * 6,
        scratch_shapes=[
            pltpu.VMEM((1024, 128), F32),
            pltpu.VMEM((128, 512), F32),
            pltpu.VMEM((64, 128), F32),
            pltpu.VMEM((128, 512), F32),
            pltpu.VMEM((64, 128), F32),
            pltpu.SemaphoreType.DMA((6,)),
        ],
        compiler_params=pltpu.CompilerParams(vmem_limit_bytes=16 * 1024 * 1024),
    )(losses, tower_all, table_all)


def solution(mesh):
    in_specs = (
        P("table", "dp", None),
        P("table", "dp", None),
        P("table", None),
        P(),
        P(),
        P(),
        P(),
        P("dp", "table"),
    )
    out_specs = (
        P("dp", "table"),
        P("table", None),
        P("table", None),
        P("table", None),
        P("table", None),
        P("table", None),
    )
    return jax.shard_map(shards, mesh=mesh, in_specs=in_specs, out_specs=out_specs, check_vma=False)
```

```python
import functools

import jax
import jax.numpy as jnp
from jax import lax
from jax.experimental import pallas as pl
from jax.experimental.pallas import tpu as pltpu
from jax.sharding import PartitionSpec as P

LOOKUPS = 8


INVERSE_TEMP = 20.0
EPSILON = 1e-06


def silu_slope(pre):
    gate = jax.nn.sigmoid(pre)
    return gate * (1.0 + pre * (1.0 - gate))


def run_tower(pooled_in, layer, head):
    pre = jnp.dot(pooled_in, layer, preferred_element_type=jnp.float32)
    hidden = jax.nn.silu(pre).astype(jnp.bfloat16)
    output = jnp.dot(hidden, head, preferred_element_type=jnp.float32)
    scale = lax.rsqrt(jnp.sum(output * output, axis=-1, keepdims=True) + EPSILON)
    return (pre, hidden, output * scale, scale)


def tower_back(d_unit, unit, scale, pre, hidden, pooled_in, head):
    along = jnp.sum(unit * d_unit, axis=-1, keepdims=True)
    d_output = ((d_unit - unit * along) * scale).astype(jnp.bfloat16)
    back = lax.dot_general(
        d_output, head, (((1,), (1,)), ((), ())), preferred_element_type=jnp.float32
    )
    d_hidden = (back * silu_slope(pre)).astype(jnp.bfloat16)
    layer_term = lax.dot_general(
        pooled_in, d_hidden, (((0,), (0,)), ((), ())), preferred_element_type=jnp.float32
    )
    head_term = lax.dot_general(
        hidden, d_output, (((0,), (0,)), ((), ())), preferred_element_type=jnp.float32
    )
    return (d_output, d_hidden, layer_term, head_term)


def input_grads(d_hidden, layer):
    return lax.dot_general(
        d_hidden, layer, (((1,), (1,)), ((), ())), preferred_element_type=jnp.float32
    ).astype(jnp.bfloat16)


def shards_general(ids, mults, table, user_layer, user_head, item_layer, item_head, counts):
    table_count = lax.axis_size("table")
    rows_dev, emb_width = table.shape
    group_rows = ids.shape[1]
    feature_count = ids.shape[2] // LOOKUPS
    own_rows = group_rows // table_count
    user_width = user_layer.shape[0]
    id_blocks = ids[0].reshape(group_rows, feature_count, LOOKUPS).transpose(1, 0, 2)
    mult_blocks = mults[0].reshape(group_rows, feature_count, LOOKUPS).transpose(1, 0, 2)
    table_rows = lax.broadcasted_iota(jnp.int32, (1, rows_dev), 1)

    def lookup_weights(id_block, mult_block):
        running = jnp.zeros((group_rows, rows_dev), jnp.float32)
        for lookup in range(LOOKUPS):
            hit = id_block[:, lookup : lookup + 1] == table_rows
            running = running + jnp.where(
                hit, mult_block[:, lookup : lookup + 1].astype(jnp.float32), 0.0
            )
        return running.astype(jnp.bfloat16)

    def pool_feature(lookup_pair):
        weights = lookup_weights(lookup_pair[0], lookup_pair[1])
        return jnp.dot(weights, table, preferred_element_type=jnp.float32).astype(jnp.bfloat16)

    partial_value = lax.map(pool_feature, (id_blocks, mult_blocks))
    received = lax.all_to_all(partial_value, "table", split_axis=1, concat_axis=1, tiled=True)
    pooled = jnp.sum(
        received.astype(jnp.float32).reshape(feature_count, table_count, own_rows, emb_width),
        axis=1,
    ).astype(jnp.bfloat16)
    pooled = pooled.transpose(1, 0, 2).reshape(own_rows, feature_count * emb_width)
    user_in = pooled[:, :user_width]
    item_in = pooled[:, user_width:]
    user_pre, user_hidden, user_unit, user_scale = run_tower(user_in, user_layer, user_head)
    item_pre, item_hidden, item_unit, item_scale = run_tower(item_in, item_layer, item_head)
    user_vector = user_unit.astype(jnp.bfloat16)
    item_vector = item_unit.astype(jnp.bfloat16)
    item_rows, item_counts = (
        lax.all_gather(item_vector, "dp", axis=0, tiled=True),
        lax.all_gather(counts[0].astype(jnp.bfloat16), "dp", axis=0, tiled=True),
    )
    log_freq = jnp.log(item_counts.astype(jnp.float32))
    scores = (
        INVERSE_TEMP
        * lax.dot_general(
            user_vector, item_rows, (((1,), (1,)), ((), ())), preferred_element_type=jnp.float32
        )
        - log_freq[None, :]
    )
    lse = jnp.log(jnp.sum(jnp.exp(scores), axis=-1))
    own_index = lax.axis_index("dp") * own_rows + lax.broadcasted_iota(jnp.int32, (own_rows,), 0)
    columns = lax.broadcasted_iota(jnp.int32, scores.shape, 1)
    is_positive = columns == own_index[:, None]
    positive = jnp.sum(jnp.where(is_positive, scores, 0.0), axis=-1)
    losses = (lse - positive)[None, :]
    dscore = (jnp.exp(scores - lse[:, None]) - is_positive.astype(jnp.float32)).astype(jnp.bfloat16)
    d_user = INVERSE_TEMP * jnp.dot(dscore, item_rows, preferred_element_type=jnp.float32)
    item_terms = INVERSE_TEMP * lax.dot_general(
        dscore, user_vector, (((0,), (0,)), ((), ())), preferred_element_type=jnp.float32
    )
    d_item = lax.psum_scatter(
        item_terms.astype(jnp.bfloat16), "dp", scatter_dimension=0, tiled=True
    ).astype(jnp.float32)
    user_dout, user_dhid, user_layer_term, user_head_term = tower_back(
        d_user, user_unit, user_scale, user_pre, user_hidden, user_in, user_head
    )
    item_dout, item_dhid, item_layer_term, item_head_term = tower_back(
        d_item, item_unit, item_scale, item_pre, item_hidden, item_in, item_head
    )
    own_grads = jnp.concatenate(
        [input_grads(user_dhid, user_layer), input_grads(item_dhid, item_layer)], axis=1
    )
    group_grads = lax.all_gather(own_grads, "table", axis=0, tiled=True)

    def add_feature(feature, running):
        weights = lookup_weights(id_blocks[feature], mult_blocks[feature])
        column = lax.dynamic_slice_in_dim(group_grads, feature * emb_width, emb_width, 1)
        return running + lax.dot_general(
            weights, column, (((0,), (0,)), ((), ())), preferred_element_type=jnp.float32
        )

    table_part = lax.fori_loop(
        0, feature_count, add_feature, jnp.zeros((rows_dev, emb_width), jnp.float32)
    )
    layer_rows = (
        lax.psum_scatter(
            user_layer_term.astype(jnp.bfloat16), "table", scatter_dimension=0, tiled=True
        ).astype(jnp.float32),
        lax.psum_scatter(
            user_head_term.astype(jnp.bfloat16), "table", scatter_dimension=0, tiled=True
        ).astype(jnp.float32),
        lax.psum_scatter(
            item_layer_term.astype(jnp.bfloat16), "table", scatter_dimension=0, tiled=True
        ).astype(jnp.float32),
        lax.psum_scatter(
            item_head_term.astype(jnp.bfloat16), "table", scatter_dimension=0, tiled=True
        ).astype(jnp.float32),
    )
    totals = (
        lax.psum(table_part.astype(jnp.bfloat16), "dp").astype(jnp.float32),
        lax.psum(layer_rows[0].astype(jnp.bfloat16), "dp").astype(jnp.float32),
        lax.psum(layer_rows[1].astype(jnp.bfloat16), "dp").astype(jnp.float32),
        lax.psum(layer_rows[2].astype(jnp.bfloat16), "dp").astype(jnp.float32),
        lax.psum(layer_rows[3].astype(jnp.bfloat16), "dp").astype(jnp.float32),
    )
    return (losses, totals[0], totals[1], totals[2], totals[3], totals[4])


BF16 = jnp.bfloat16
F32 = jnp.float32
ROW_ID = jnp.int16
CHUNKS = 4
MESH = pl.DeviceIdType.MESH


def flip(value, mask, bits):
    out = 0
    for bit in range(bits):
        one = lax.rem(lax.div(value, 1 << bit), 2)
        if (mask >> bit) & 1:
            one = 1 - one
        out = out + one * (1 << bit)
    return out


def dot_nt(left, right):
    return lax.dot_general(left, right, (((1,), (1,)), ((), ())), preferred_element_type=F32)


def dot_tn(left, right):
    return lax.dot_general(left, right, (((0,), (0,)), ((), ())), preferred_element_type=F32)


def step_kernel(
    ids_hbm,
    mults_hbm,
    table_hbm,
    user_layer_hbm,
    user_head_hbm,
    item_layer_hbm,
    item_head_hbm,
    counts_hbm,
    losses_ref,
    tower_all,
    table_all,
    ids_ref,
    mults_ref,
    table_ref,
    user_layer_ref,
    user_head_ref,
    item_layer_ref,
    item_head_ref,
    counts_ref,
    user_layer_t,
    user_head_t,
    item_layer_t,
    item_head_t,
    ids_t,
    mults_t,
    table_t,
    row_ids,
    weights,
    parts,
    pair_in,
    sums,
    sums_in,
    slices,
    slices_in,
    units,
    grads,
    tower_terms,
    tower_in,
    tower_mid,
    tower_second,
    table_terms,
    table_in,
    table_mid,
    table_second,
    load_sems,
    pair_sems,
    sums_sems,
    slices_sems,
    units_sems,
    grads_sems,
    pass_sems,
    tower_sems,
    tower_all_sems,
    table_sems,
    table_all_sems,
):
    pairs = (
        (ids_hbm, ids_ref),
        (mults_hbm, mults_ref),
        (table_hbm, table_ref),
        (user_layer_hbm, user_layer_ref),
        (item_layer_hbm, item_layer_ref),
        (user_head_hbm, user_head_ref),
        (item_head_hbm, item_head_ref),
        (counts_hbm, counts_ref),
    )
    loads = [pltpu.make_async_copy(a, b, load_sems.at[i]) for i, (a, b) in enumerate(pairs)]
    for load in loads:
        load.start()
    t = lax.axis_index("table")
    d = lax.axis_index("dp")
    z = lax.div(t, 2)
    core = lax.rem(t, 2)
    sibling = z * 2 + (1 - core)
    z_peers = [flip(z, k, 2) for k in range(4)]
    dp_peers = [flip(d, k, 2) for k in range(4)]

    barrier = pltpu.get_barrier_semaphore()
    for k in range(1, 8):
        pl.semaphore_signal(barrier, inc=1, device_id={"table": flip(t, k, 3)}, device_id_type=MESH)
    for k in range(1, 4):
        pl.semaphore_signal(barrier, inc=1, device_id={"dp": dp_peers[k]}, device_id_type=MESH)

    def send(src, dst, sems, index, target):
        copy = pltpu.make_async_remote_copy(
            src_ref=src,
            dst_ref=dst,
            send_sem=sems.at[0, index],
            recv_sem=sems.at[1, index],
            device_id=target,
            device_id_type=MESH,
        )
        copy.start()
        return copy

    row_ids[...] = lax.broadcasted_iota(jnp.int32, row_ids.shape, 0).astype(row_ids.dtype)
    for load in loads[:3]:
        load.wait()
    ids_t[...] = ids_ref[...].T
    mults_t[...] = mults_ref[...].T
    table_t[...] = table_ref[...].T
    block = 128

    def pool_pair(chunk, pair):
        for half in range(2):
            feature = chunk * 4 + pair * 2 + half
            slots = pl.ds(pl.multiple_of(feature * 8, 8), 8)
            id_rows = ids_t[slots, :]
            mult_rows = mults_t[slots, :].astype(F32)
            spread = [
                (
                    jnp.broadcast_to(id_rows[l : l + 1, :], (16, 128)).astype(row_ids.dtype),
                    jnp.broadcast_to(mult_rows[l : l + 1, :], (16, 128)).astype(BF16),
                )
                for l in range(LOOKUPS)
            ]
            lanes = pl.ds(pl.multiple_of(feature * 128, 128), 128)
            for start in range(0, 1024, block):
                here = row_ids[start : start + block, :].reshape(block // 16, 16, 128)
                total = None
                for id_row, mult_row in spread:
                    term = jnp.where(here == id_row[None], mult_row[None], jnp.zeros((), BF16))
                    total = term if total is None else total + term
                weights[start : start + block, lanes] = total.reshape(block, 128)
        lanes = pl.ds(pl.multiple_of((chunk * 4 + pair * 2) * 128, 256), 256)
        pooled_t = jnp.dot(table_t[...], weights[:, lanes], preferred_element_type=F32)
        for half in range(2):
            pooled = pooled_t[:, half * 128 : half * 128 + 128].T.astype(BF16)
            place = pl.ds(pl.multiple_of((pair * 2 + half) * 128, 128), 128)
            for owner in range(8):
                parts[chunk, owner % 2, owner // 2, :, place] = pooled[owner * 16 : owner * 16 + 16]

    pair_copies, sums_copies = [], []

    def pass_on(chunk):
        pair_copies[chunk].wait_recv()
        total = parts[chunk, core].astype(F32) + pair_in[chunk].astype(F32)
        sums[chunk] = total.astype(BF16)
        for k in range(1, 4):
            sums_copies.append(
                send(
                    sums.at[chunk, z_peers[k]],
                    sums_in.at[chunk, k - 1],
                    sums_sems,
                    chunk * 3 + k - 1,
                    {"table": z_peers[k] * 2 + core},
                )
            )

    for chunk in range(CHUNKS):

        def pool_step(pair, carry):
            pool_pair(chunk, pair)
            return carry

        lax.fori_loop(0, 2, pool_step, 0)
        if chunk == 0:
            pl.semaphore_wait(barrier, 10)
        pair_copies.append(
            send(
                parts.at[chunk, 1 - core],
                pair_in.at[chunk],
                pair_sems,
                chunk,
                {"table": sibling},
            )
        )
        if chunk > 0:
            pass_on(chunk - 1)
    for load in loads[3:]:
        load.wait()
    pass_on(CHUNKS - 1)

    def pooled_chunk(chunk):
        total = sums[chunk, z].astype(F32)
        for k in range(3):
            sums_copies[chunk * 3 + k].wait_recv()
            total = total + sums_in[chunk, k].astype(F32)
        return total.astype(BF16)

    user_in = jnp.concatenate([pooled_chunk(0), pooled_chunk(1)], axis=1)
    user_pre, user_hidden, user_unit, user_scale = run_tower(
        user_in, user_layer_ref[...], user_head_ref[...]
    )
    item_in = jnp.concatenate([pooled_chunk(2), pooled_chunk(3)], axis=1)
    item_pre, item_hidden, item_unit, item_scale = run_tower(
        item_in, item_layer_ref[...], item_head_ref[...]
    )
    eye16 = lax.broadcasted_iota(jnp.int32, (16, 16), 0) == lax.broadcasted_iota(
        jnp.int32, (16, 16), 1
    )
    count_column = jnp.sum(
        jnp.where(eye16, jnp.broadcast_to(counts_ref[...].astype(F32), (16, 16)), 0.0),
        axis=1,
        keepdims=True,
    )
    units[0, :, 0:128] = user_unit.astype(BF16)
    units[0, :, 128:256] = item_unit.astype(BF16)
    units[0, :, 256:384] = jnp.broadcast_to(count_column, (16, 128)).astype(BF16)
    units_copies = [
        send(units.at[0], units.at[k], units_sems, k - 1, {"dp": dp_peers[k]}) for k in range(1, 4)
    ]
    for owner in range(8):
        slices[owner, :, 0:128] = user_in[:, owner * 128 : owner * 128 + 128]
        slices[owner, :, 128:256] = item_in[:, owner * 128 : owner * 128 + 128]
        slices[owner, :, 256:384] = jnp.concatenate(
            [
                user_hidden[:, owner * 64 : owner * 64 + 64],
                item_hidden[:, owner * 64 : owner * 64 + 64],
            ],
            axis=1,
        )
    slices_copies = []
    for k in range(1, 8):
        peer = flip(t, k, 3)
        slices_copies.append(
            send(slices.at[peer], slices_in.at[t], slices_sems, k - 1, {"table": peer})
        )
    slices_in[t] = slices[t]
    user_head_t[...] = user_head_ref[...].T
    item_head_t[...] = item_head_ref[...].T
    for copy in units_copies:
        copy.wait_recv()

    every = units[...]
    users = every[:, :, 0:128].reshape(64, 128)
    items = every[:, :, 128:256].reshape(64, 128)
    log_freq = jnp.log(every[:, :, 256:384].reshape(64, 128).astype(F32))[:, 0:1]
    scores = INVERSE_TEMP * dot_nt(items, users) - log_freq
    lse = jnp.log(jnp.sum(jnp.exp(scores), axis=0, keepdims=True))
    same = lax.broadcasted_iota(jnp.int32, (64, 64), 0) == lax.broadcasted_iota(
        jnp.int32, (64, 64), 1
    )
    positive = jnp.sum(jnp.where(same, scores, 0.0), axis=0, keepdims=True)
    losses_ref[...] = (lse - positive)[:, 0:16]
    dscore = (jnp.exp(scores - lse) - jnp.where(same, 1.0, 0.0)).astype(BF16)
    d_user = INVERSE_TEMP * dot_tn(dscore, items)[0:16]
    d_item = INVERSE_TEMP * jnp.dot(dscore[0:16], users, preferred_element_type=F32)

    def back(d_unit, unit, scale, pre, head_t):
        along = jnp.sum(unit * d_unit, axis=-1, keepdims=True)
        d_output = ((d_unit - unit * along) * scale).astype(BF16)
        d_hidden = (
            jnp.dot(d_output, head_t[...], preferred_element_type=F32) * silu_slope(pre)
        ).astype(BF16)
        return d_output, d_hidden

    user_dout, user_dhid = back(d_user, user_unit, user_scale, user_pre, user_head_t)
    item_dout, item_dhid = back(d_item, item_unit, item_scale, item_pre, item_head_t)
    grads[t] = jnp.concatenate([user_dhid, item_dhid, user_dout, item_dout], axis=1)
    grads_copies = [
        send(
            grads.at[t], grads.at[t], grads_sems, k - 1, {"table": z_peers[k] * 2 + core}
        )
        for k in range(1, 4)
    ]
    pass_copies = [send(grads.at[t], grads.at[t], pass_sems, 0, {"table": sibling})]
    user_layer_t[...] = user_layer_ref[...].T
    item_layer_t[...] = item_layer_ref[...].T
    for k in range(1, 4):
        grads_copies[k - 1].wait_recv()
        slot = z_peers[k] * 2 + core
        pass_copies.append(
            send(grads.at[slot], grads.at[slot], pass_sems, k, {"table": sibling})
        )
    for copy in pass_copies:
        copy.wait_recv()
    for copy in slices_copies:
        copy.wait_recv()

    every = grads[...].reshape(128, 1280)
    kept = slices_in[...].reshape(128, 384)
    user_rows = dot_tn(kept[:, 0:128], every[:, 0:512]).astype(BF16)
    item_rows = dot_tn(kept[:, 128:256], every[:, 512:1024]).astype(BF16)
    head_rows = dot_tn(kept[:, 256:384], every[:, 1024:1280]).astype(BF16)
    for part in range(4):
        lanes = slice(part * 128, part * 128 + 128)
        tower_terms[part, 0, 0:128, :] = user_rows[:, lanes]
        tower_terms[part, 0, 128:144, :] = head_rows[part * 16 : part * 16 + 16, 0:128]
        tower_terms[part, 1, 0:128, :] = item_rows[:, lanes]
        tower_terms[part, 1, 128:144, :] = head_rows[64 + part * 16 : 80 + part * 16, 128:256]

    by_x, by_y, across = dp_peers[1], dp_peers[2], dp_peers[3]

    def scatter_start(terms, first, sems):
        return [
            send(terms.at[across, 0], first.at[0, 1], sems, 0, {"dp": by_x}),
            send(terms.at[across, 1], first.at[1, 1], sems, 1, {"dp": by_y}),
            send(terms.at[by_x, 0], first.at[0, 0], sems, 2, {"dp": by_x}),
            send(terms.at[by_y, 1], first.at[1, 0], sems, 3, {"dp": by_y}),
        ]

    def scatter_pass(terms, first, middle, second, copies, sems):
        for half, target in ((0, by_y), (1, by_x)):
            copies[half].wait_recv()
            total = terms[target, half].astype(F32) + first[half, 1].astype(F32)
            middle[half] = total.astype(BF16)
            copies.append(
                send(middle.at[half], second.at[half], sems, 4 + half, {"dp": target})
            )

    def gather_start(terms, first, second, copies, result, sems):
        for half in range(2):
            copies[2 + half].wait_recv()
            copies[4 + half].wait_recv()
            total = terms[d, half].astype(F32) + first[half, 0].astype(F32)
            result[d, half] = (total + second[half].astype(F32)).astype(BF16)
        own = [result.at[d, 0], result.at[d, 1]]
        return [
            send(own[0], own[0], sems, 0, {"dp": by_y}),
            send(own[1], own[1], sems, 1, {"dp": by_x}),
            send(own[0], own[0], sems, 2, {"dp": by_x}),
            send(own[1], own[1], sems, 3, {"dp": by_y}),
        ]

    def gather_pass(copies, result, sems):
        for half, source, target in ((0, by_y, by_x), (1, by_x, by_y)):
            copies[half].wait_recv()
            held = result.at[source, half]
            copies.append(send(held, held, sems, 4 + half, {"dp": target}))

    tower_copies = scatter_start(tower_terms, tower_in, tower_sems)

    user_dpool = jnp.dot(
        every[:, 0:512], user_layer_t[...], preferred_element_type=F32
    ).astype(BF16)
    item_dpool = jnp.dot(
        every[:, 512:1024], item_layer_t[...], preferred_element_type=F32
    ).astype(BF16)
    columns = [user_dpool[:, f * 128 : f * 128 + 128] for f in range(8)] + [
        item_dpool[:, f * 128 : f * 128 + 128] for f in range(8)
    ]
    d_pooled = jnp.concatenate(columns, axis=0)
    for part in range(4):
        table_terms[part] = (
            jnp.dot(
                weights[part * 256 : part * 256 + 256, :], d_pooled, preferred_element_type=F32
            )
            .astype(BF16)
            .reshape(2, 128, 128)
        )
    table_copies = scatter_start(table_terms, table_in, table_sems)
    scatter_pass(tower_terms, tower_in, tower_mid, tower_second, tower_copies, tower_sems)
    scatter_pass(table_terms, table_in, table_mid, table_second, table_copies, table_sems)
    tower_all_copies = gather_start(
        tower_terms, tower_in, tower_second, tower_copies, tower_all, tower_all_sems
    )
    table_all_copies = gather_start(
        table_terms, table_in, table_second, table_copies, table_all, table_all_sems
    )
    gather_pass(tower_all_copies, tower_all, tower_all_sems)
    gather_pass(table_all_copies, table_all, table_all_sems)
    for copy in tower_all_copies[2:] + table_all_copies[2:]:
        copy.wait_recv()
    for copy in (
        pair_copies
        + sums_copies
        + units_copies
        + slices_copies
        + grads_copies
        + pass_copies
        + tower_copies
        + table_copies
        + tower_all_copies
        + table_all_copies
    ):
        copy.wait_send()


def finish_kernel(
    losses_ref,
    tower_ref,
    table_ref,
    losses_out,
    table_out,
    user_layer_out,
    user_head_out,
    item_layer_out,
    item_head_out,
    table_wide,
    user_layer_wide,
    user_head_wide,
    item_layer_wide,
    item_head_wide,
    sems,
):
    copies = []

    def put(src, dst):
        copies.append(pltpu.make_async_copy(src, dst, sems.at[len(copies)]))
        copies[-1].start()

    put(losses_ref, losses_out)
    for part in range(4):
        table_wide[part * 256 : part * 256 + 256, :] = table_ref[part].reshape(256, 128).astype(F32)
    put(table_wide, table_out)
    for part in range(4):
        lanes = slice(part * 128, part * 128 + 128)
        user_layer_wide[:, lanes] = tower_ref[part, 0, 0:128, :].astype(F32)
    put(user_layer_wide, user_layer_out)
    for part in range(4):
        lanes = slice(part * 128, part * 128 + 128)
        item_layer_wide[:, lanes] = tower_ref[part, 1, 0:128, :].astype(F32)
    put(item_layer_wide, item_layer_out)
    for part in range(4):
        rows = slice(part * 16, part * 16 + 16)
        user_head_wide[rows, :] = tower_ref[part, 0, 128:144, :].astype(F32)
        item_head_wide[rows, :] = tower_ref[part, 1, 128:144, :].astype(F32)
    put(user_head_wide, user_head_out)
    put(item_head_wide, item_head_out)
    for copy in copies:
        copy.wait()


def shards(ids, mults, table, user_layer, user_head, item_layer, item_head, counts):
    small = lax.axis_size("table") == 8 and lax.axis_size("dp") == 4
    if not small or ids.shape != (1, 128, 128) or table.shape != (1024, 128):
        return shards_general(
            ids, mults, table, user_layer, user_head, item_layer, item_head, counts
        )

    def dma(count):
        return pltpu.SemaphoreType.DMA((2, count))

    held = [
        pltpu.with_memory_space_constraint(x, pltpu.HBM)
        for x in (ids[0], mults[0], table, user_layer, user_head, item_layer, item_head, counts)
    ]
    vmem = pl.BlockSpec(memory_space=pltpu.VMEM)
    hbm = pl.BlockSpec(memory_space=pltpu.HBM)
    losses, tower_all, table_all = pl.pallas_call(
        step_kernel,
        out_shape=(
            jax.ShapeDtypeStruct((1, 16), F32),
            jax.ShapeDtypeStruct((4, 2, 144, 128), BF16),
            jax.ShapeDtypeStruct((4, 2, 128, 128), BF16),
        ),
        in_specs=[hbm] * 8,
        out_specs=(vmem,) * 3,
        scratch_shapes=[
            pltpu.VMEM((128, 128), jnp.int32),
            pltpu.VMEM((128, 128), jnp.int32),
            pltpu.VMEM((1024, 128), BF16),
            pltpu.VMEM((1024, 512), BF16),
            pltpu.VMEM((512, 128), BF16),
            pltpu.VMEM((1024, 512), BF16),
            pltpu.VMEM((512, 128), BF16),
            pltpu.VMEM((1, 16), jnp.int32),
            pltpu.VMEM((512, 1024), BF16),
            pltpu.VMEM((128, 512), BF16),
            pltpu.VMEM((512, 1024), BF16),
            pltpu.VMEM((128, 512), BF16),
            pltpu.VMEM((128, 128), jnp.int32),
            pltpu.VMEM((128, 128), jnp.int32),
            pltpu.VMEM((128, 1024), BF16),
            pltpu.VMEM((1024, 128), ROW_ID),
            pltpu.VMEM((1024, 2048), BF16),
            pltpu.VMEM((CHUNKS, 2, 4, 16, 512), BF16),
            pltpu.VMEM((CHUNKS, 4, 16, 512), BF16),
            pltpu.VMEM((CHUNKS, 4, 16, 512), BF16),
            pltpu.VMEM((CHUNKS, 3, 16, 512), BF16),
            pltpu.VMEM((8, 16, 384), BF16),
            pltpu.VMEM((8, 16, 384), BF16),
            pltpu.VMEM((4, 16, 384), BF16),
            pltpu.VMEM((8, 16, 1280), BF16),
            pltpu.VMEM((4, 2, 144, 128), BF16),
            pltpu.VMEM((2, 2, 144, 128), BF16),
            pltpu.VMEM((2, 144, 128), BF16),
            pltpu.VMEM((2, 144, 128), BF16),
            pltpu.VMEM((4, 2, 128, 128), BF16),
            pltpu.VMEM((2, 2, 128, 128), BF16),
            pltpu.VMEM((2, 128, 128), BF16),
            pltpu.VMEM((2, 128, 128), BF16),
            pltpu.SemaphoreType.DMA((8,)),
            dma(CHUNKS),
            dma(CHUNKS * 3),
            dma(7),
            dma(3),
            dma(3),
            dma(4),
            dma(6),
            dma(6),
            dma(6),
            dma(6),
        ],
        compiler_params=pltpu.CompilerParams(
            collective_id=0, has_side_effects=True, vmem_limit_bytes=40 * 1024 * 1024
        ),
        cost_estimate=pl.CostEstimate(
            flops=3_000_000_000, bytes_accessed=4_500_000, transcendentals=100_000
        ),
    )(*held)
    return pl.pallas_call(
        finish_kernel,
        out_shape=(
            jax.ShapeDtypeStruct((1, 16), F32),
            jax.ShapeDtypeStruct((1024, 128), F32),
            jax.ShapeDtypeStruct((128, 512), F32),
            jax.ShapeDtypeStruct((64, 128), F32),
            jax.ShapeDtypeStruct((128, 512), F32),
            jax.ShapeDtypeStruct((64, 128), F32),
        ),
        in_specs=[vmem] * 3,
        out_specs=(hbm,) * 6,
        scratch_shapes=[
            pltpu.VMEM((1024, 128), F32),
            pltpu.VMEM((128, 512), F32),
            pltpu.VMEM((64, 128), F32),
            pltpu.VMEM((128, 512), F32),
            pltpu.VMEM((64, 128), F32),
            pltpu.SemaphoreType.DMA((6,)),
        ],
        compiler_params=pltpu.CompilerParams(vmem_limit_bytes=16 * 1024 * 1024),
    )(losses, tower_all, table_all)


def solution(mesh):
    in_specs = (
        P("table", "dp", None),
        P("table", "dp", None),
        P("table", None),
        P(),
        P(),
        P(),
        P(),
        P("dp", "table"),
    )
    out_specs = (
        P("dp", "table"),
        P("table", None),
        P("table", None),
        P("table", None),
        P("table", None),
        P("table", None),
    )
    return jax.shard_map(shards, mesh=mesh, in_specs=in_specs, out_specs=out_specs, check_vma=False)
```
